128 devices in a mesh: row: 32 (over x, y_lo, z), frame: 4 (over y_hi, core).
Axes of the slice: x: 4, y: 4 (y_hi: 2, y_lo: 2; y = y_hi * 2 + y_lo), z: 4, core: 2. Of those that a mesh axis runs over, the one named last changes fastest.
Arguments:
- latent: bfloat16 [4, 64, 240, 384], P('frame', 'row'), may hold values from -6 to 6
- cache_first: bfloat16 [2, 64, 240, 384], P(None, 'row'), may hold values from -6 to 6
- cache_second: bfloat16 [2, 64, 240, 384], P(None, 'row'), may hold values from -6 to 6
- gain_first: float32 [384], replicated, may hold values from 0.5 to 2
- conv_first: bfloat16 [3, 3, 3, 384, 384], replicated, may hold values from -0.0625 to 0.0625
- gain_second: float32 [384], replicated, may hold values from 0.5 to 2
- conv_second: bfloat16 [3, 3, 3, 384, 384], replicated, may hold values from -0.0625 to 0.0625
- gain_attention: float32 [384], replicated, may hold values from 0.5 to 2
- query_weight: bfloat16 [384, 384], replicated, may hold values from -3 to 3
- keyvalue_weight: bfloat16 [384, 768], replicated, may hold values from -0.3125 to 0.3125
- out_weight: bfloat16 [384, 384], replicated, may hold values from -0.3125 to 0.3125
Outputs:
- mixed: float32 [4, 64, 240, 384], P('frame', 'row')
The draws below stay inside these ranges and needn't reach their ends.
All inputs are finite; a program needn't handle non-finite values.
Results may differ from the reference program's by a relative error of at most 0.039.
The reference program's roundings to bfloat16 on the way (of `activated`, `hidden`, `normed`, `weights` and `attended`) count: a program that leaves them out, or rounds other values in their place, can miss the bound.
Values may be sent and summed in bfloat16 or wider, within the bound.
No kernel may reach another device: no remote copies, remote signals or barrier semaphores. Data moves between devices by JAX's collectives and lax.ppermute only.
A program may use at most 192 MiB of HBM per device.

```python
import math
import jax
import jax.numpy as jnp
from jax import lax

C = 384
W = 240
ROWS_DEV = 2
H = 64
FRAMES = 4


def draw_query_weight(key, part):
    key = jax.random.fold_in(key, 7)
    values = jnp.clip(jax.random.normal(key, (C, C), jnp.float32) * (2.5 / math.sqrt(C)), -3.0, 3.0)
    return values.astype(jnp.bfloat16)


def level_of(stream_key, dims, split, low, high):
    loudness, own = 1.0, jax.random.fold_in(stream_key, 6)
    for axis_at, blocks in split:
        steps = jnp.exp(jax.random.uniform(jax.random.fold_in(own, axis_at), (blocks,), jnp.float32, low / len(split), high / len(split)))
        loudness = loudness * jnp.repeat(steps, dims[axis_at] // blocks).reshape([-1 if axis == axis_at else 1 for axis in range(len(dims))])
    return loudness


def scatter_about(key, shape, scale, bound, cuts=(), kind=jnp.bfloat16):
    values = jax.random.normal(key, shape, jnp.float32) * scale
    if len(cuts) > 0:
        values = level_of(key, shape, cuts, -0.22, 0.18) * values
    return jnp.clip(values, min=-bound, max=bound).astype(kind)


def setup_inputs(seed: int = 0) -> dict:
    key_of = jax.random.split(jax.random.key(seed), 12)
    latent = scatter_about(key_of[0], (FRAMES, H, W, C), 1.0, 6.0, ((0, 4), (1, 32)))
    cache_first = scatter_about(key_of[1], (2, H, W, C), 1.0, 6.0, ((1, 32),))
    cache_second = scatter_about(key_of[2], (2, H, W, C), 1.0, 6.0, ((1, 32),))
    gain_first = jnp.clip(jnp.exp(jax.random.uniform(key_of[3], (C,), jnp.float32, math.log(0.5), math.log(2.0))), 0.5, 2.0)
    conv_first = scatter_about(key_of[4], (3, 3, 3, C, C), (27 * C) ** -0.5, 0.0625)
    gain_second = jnp.clip(jnp.exp(jax.random.uniform(key_of[5], (C,), jnp.float32, math.log(0.5), math.log(2.0))), 0.5, 2.0)
    conv_second = scatter_about(key_of[6], (3, 3, 3, C, C), (27 * C) ** -0.5, 0.0625)
    gain_attention = jnp.clip(jnp.exp(jax.random.uniform(key_of[7], (C,), jnp.float32, math.log(0.5), math.log(2.0))), 0.5, 2.0)
    query_weight = draw_query_weight(jax.random.fold_in(key_of[11], 71), 0)
    keyvalue_weight = scatter_about(key_of[9], (C, 2 * C), C ** -0.5, 0.3125)
    out_weight = scatter_about(key_of[10], (C, C), C ** -0.5, 0.3125)
    return {"latent": latent, "cache_first": cache_first, "cache_second": cache_second, "gain_first": gain_first, "conv_first": conv_first, "gain_second": gain_second, "conv_second": conv_second, "gain_attention": gain_attention, "query_weight": query_weight, "keyvalue_weight": keyvalue_weight, "out_weight": out_weight}


def root_norm(tensor, scaling):
    widened = tensor.astype(jnp.float32)
    return widened * lax.rsqrt(lax.optimization_barrier(jnp.mean(widened * widened, axis=-1, keepdims=True)) + 1e-06) * scaling

def causal_conv(cache_frames, inputs, weight):
    extended = jnp.concatenate([cache_frames, inputs], axis=0)[None]
    result = lax.conv_general_dilated(extended, weight, (1, 1, 1), ((0, 0), (1, 1), (1, 1)), dimension_numbers=('NDHWC', 'DHWIO', 'NDHWC'), preferred_element_type=jnp.float32)
    return result[0]

def reference(latent, cache_first, cache_second, gain_first, conv_first, gain_second, conv_second, gain_attention, query_weight, keyvalue_weight, out_weight):
    activated = jax.nn.silu(root_norm(latent, gain_first)).astype(jnp.bfloat16)
    first_out = causal_conv(cache_first, activated, conv_first)
    hidden = jax.nn.silu(root_norm(first_out, gain_second)).astype(jnp.bfloat16)
    second_out = causal_conv(cache_second, hidden, conv_second)
    residual = latent.astype(jnp.float32) + second_out
    normed = root_norm(residual, gain_attention).astype(jnp.bfloat16)
    flattened = normed.reshape(-1, C)
    queries = jnp.dot(flattened, query_weight, preferred_element_type=jnp.float32).astype(jnp.bfloat16)
    key_value = jnp.dot(flattened, keyvalue_weight, preferred_element_type=jnp.float32).astype(jnp.bfloat16)
    frames_total = latent.shape[0]
    queries = queries.reshape(frames_total, -1, C)
    key_rows = key_value[:, :C].reshape(frames_total, -1, C)
    value_rows = key_value[:, C:].reshape(frames_total, -1, C)
    score_scale = 1.0 / math.sqrt(C)
    block_size = ROWS_DEV * W

    def attend_frame(tensors):
        frame_queries, frame_keys, frame_values = tensors

        def attend_block(query_block):
            scores = jnp.dot(query_block, frame_keys.T, preferred_element_type=jnp.float32) * score_scale
            peak = lax.optimization_barrier(jnp.max(scores, axis=-1, keepdims=True))
            exponent = jnp.exp(scores - peak)
            denominator = lax.optimization_barrier(jnp.sum(exponent, axis=-1, keepdims=True))
            weights = exponent.astype(jnp.bfloat16)
            return (jnp.dot(weights, frame_values, preferred_element_type=jnp.float32) / denominator).astype(jnp.bfloat16)
        blocks = frame_queries.reshape(-1, block_size, C)
        return lax.map(attend_block, blocks).reshape(-1, C)
    attended = lax.map(attend_frame, (queries, key_rows, value_rows)).reshape(-1, C)
    projected = jnp.dot(attended, out_weight, preferred_element_type=jnp.float32)
    return residual + projected.reshape(residual.shape)
```

```python
import functools
import math

import jax
import jax.numpy as jnp
from jax import lax
from jax.experimental import pallas as pl
from jax.experimental.pallas import tpu as pltpu
from jax.sharding import Mesh
from jax.sharding import PartitionSpec as P

C = 384
COLS = 60
WIDE = 64
ROWS = 2
SLICE = ROWS * COLS
BLOCK = 4 * SLICE
HALF = BLOCK // 2
AXES = ("x", "yl", "z", "yh", "c")
SIZES = {"x": 4, "yl": 2, "z": 4, "yh": 2, "c": 2}
BF = jnp.bfloat16
F32 = jnp.float32
SCALE = math.log2(math.e) / math.sqrt(C)


def routes(axes, target):
    sizes = [SIZES[a] for a in axes]
    total = math.prod(sizes)
    pairs = []
    for source in range(total):
        rest, where = source, {}
        for a, n in zip(reversed(axes), reversed(sizes)):
            where[a] = rest % n
            rest //= n
        there = target(dict(where))
        if there is None:
            continue
        index = 0
        for a, n in zip(axes, sizes):
            index = index * n + there[a] % n
        pairs.append((source, index))
    return pairs


def send(value, axes, target):
    return lax.ppermute(value, axes, routes(axes, target))


def neighbour(dr, k):
    def target(w):
        row = (w["x"] * 2 + w["yl"]) * 4 + w["z"] + dr
        if row < 0 or row > 31:
            return None
        member = (w["yh"] * 2 + w["c"]) ^ k
        return {
            "x": row // 8, "yl": row // 4 % 2, "z": row % 4,
            "yh": member // 2, "c": member % 2,
        }

    return target


def to_plane(k):
    def target(w):
        frame = (w["yh"] * 2 + w["c"]) ^ k
        return {"yh": frame // 2, "yl": frame % 2, "c": w["yl"]}

    return target


def along(step, key_line):
    def target(w):
        axis = "x" if (w["c"] == 0) == key_line else "z"
        w[axis] += step
        return w

    return target


def to_home(j):
    return lambda w: {"yl": w["c"] ^ j, "c": w["yl"]}


def norm(v, gain):
    return v * lax.rsqrt(jnp.mean(v * v, axis=-1, keepdims=True) + 1e-06) * gain


def silu(v):
    return v / (1.0 + jnp.exp(-v))


def taps(t, frames, w_ref, acc):
    xs = frames[pl.ds(t, 4)]
    lhs = jnp.concatenate([xs[:, r : r + ROWS] for r in range(3)], axis=-1)
    lhs = lhs.reshape(4 * ROWS * WIDE, 3 * C)
    rhs = jnp.concatenate([w_ref[0, :, c].reshape(3 * C, C) for c in range(3)], axis=-1)
    y = jnp.dot(lhs, rhs, preferred_element_type=F32)

    @pl.when(t == 0)
    def _():
        acc[...] = y

    @pl.when(t > 0)
    def _():
        acc[...] += y


def summed(y):
    n = y.shape[0]
    return (
        pltpu.roll(y[:, :C], 1, 0) + y[:, C : 2 * C] + pltpu.roll(y[:, 2 * C :], n - 1, 0)
    )


def conv_first_kernel(
    q_ref, o0, o1, o2, o3, u0, u1, u2, u3, d0, d1, d2, d3, c_ref, cu_ref, cd_ref,
    g1_ref, g2_ref, w_ref, out_ref, frames, acc,
):
    t = pl.program_id(0)
    q = q_ref[0]

    @pl.when(t == 0)
    def _():
        frames[0:2, 0:1] = cu_ref[...]
        frames[0:2, 1:3] = c_ref[...]
        frames[0:2, 3:4] = cd_ref[...]
        gain = g1_ref[...].reshape(1, 1, C)
        for k, (up, own, down) in enumerate(zip((u0, u1, u2, u3), (o0, o1, o2, o3), (d0, d1, d2, d3))):
            f = 2 + (q ^ k)
            frames[f, 0:1] = silu(norm(up[...].astype(F32), gain)).astype(BF)
            frames[f, 1:3] = silu(norm(own[...].astype(F32), gain)).astype(BF)
            frames[f, 3:4] = silu(norm(down[...].astype(F32), gain)).astype(BF)

    taps(t, frames, w_ref, acc)

    @pl.when(t == 2)
    def _():
        place = lax.broadcasted_iota(jnp.int32, (WIDE, 1), 0)
        column = place + COLS * q - 2
        valid = (column >= 0) & (column < 4 * COLS) & (place > 0) & (place < WIDE - 1)
        for f in range(4):
            y = summed(acc[f * ROWS * WIDE : (f + 1) * ROWS * WIDE])
            h = silu(norm(y, g2_ref[...])).reshape(ROWS, WIDE, C)
            out_ref[f] = jnp.where(valid[None], h, 0.0).astype(BF)


def conv_second_kernel(
    q_ref, h_ref, hu_ref, hd_ref, c_ref, cu_ref, cd_ref, o0, o1, o2, o3, g_ref, w_ref,
    n0, n1, n2, n3, r0, r1, r2, r3, frames, acc,
):
    t = pl.program_id(0)
    q = q_ref[0]

    @pl.when(t == 0)
    def _():
        frames[0:2, 0:1] = cu_ref[...]
        frames[0:2, 1:3] = c_ref[...]
        frames[0:2, 3:4] = cd_ref[...]
        frames[2:6, 0:1] = hu_ref[...]
        frames[2:6, 1:3] = h_ref[...]
        frames[2:6, 3:4] = hd_ref[...]

    taps(t, frames, w_ref, acc)

    @pl.when(t == 2)
    def _():
        span = ROWS * WIDE
        for k, (own, n_ref, r_ref) in enumerate(zip((o0, o1, o2, o3), (n0, n1, n2, n3), (r0, r1, r2, r3))):
            f = q ^ k
            y = summed(acc[pl.ds(pl.multiple_of(f * span, span), span)])
            total = y + own[...].astype(F32).reshape(span, C)
            total = pltpu.roll(total, span - 2, 0)
            kept = jnp.concatenate([total[0:COLS], total[WIDE : WIDE + COLS]], axis=0)
            r_ref[...] = kept
            n_ref[...] = norm(kept, g_ref[...]).astype(BF)


def conv_scratch():
    return [
        pltpu.VMEM((6, 4, WIDE, C), BF),
        pltpu.VMEM((4 * ROWS * WIDE, 3 * C), F32),
    ]


def whole(*shape):
    return pl.BlockSpec(shape, lambda *_: (0,) * len(shape))


SCALAR = pl.BlockSpec(memory_space=pltpu.SMEM)
TAPS = pl.BlockSpec((1, 3, 3, C, C), lambda t: (t, 0, 0, 0, 0))
PARAMS = pltpu.CompilerParams(vmem_limit_bytes=40 * 1024 * 1024)


def conv_first_call(q, own, up, down, cache, gain1, gain2, weight):
    return pl.pallas_call(
        conv_first_kernel,
        grid=(3,),
        out_shape=jax.ShapeDtypeStruct((4, ROWS, WIDE, C), BF),
        in_specs=[SCALAR]
        + [whole(ROWS, WIDE, C)] * 4
        + [whole(1, WIDE, C)] * 8
        + [whole(2, ROWS, WIDE, C), whole(2, 1, WIDE, C), whole(2, 1, WIDE, C)]
        + [whole(1, C), whole(1, C), TAPS],
        out_specs=whole(4, ROWS, WIDE, C),
        scratch_shapes=conv_scratch(),
        compiler_params=PARAMS,
        name="conv_first",
    )(q, *own, *up, *down, *cache, gain1, gain2, weight)


def conv_second_call(q, hidden, up, down, cache, own, gain, weight):
    return pl.pallas_call(
        conv_second_kernel,
        grid=(3,),
        out_shape=[jax.ShapeDtypeStruct((SLICE, C), BF)] * 4
        + [jax.ShapeDtypeStruct((SLICE, C), F32)] * 4,
        in_specs=[SCALAR]
        + [whole(4, ROWS, WIDE, C), whole(4, 1, WIDE, C), whole(4, 1, WIDE, C)]
        + [whole(2, ROWS, WIDE, C), whole(2, 1, WIDE, C), whole(2, 1, WIDE, C)]
        + [whole(ROWS, WIDE, C)] * 4
        + [whole(1, C), TAPS],
        out_specs=[whole(SLICE, C)] * 8,
        scratch_shapes=conv_scratch(),
        compiler_params=PARAMS,
        name="conv_second",
    )(q, hidden, up, down, *cache, *own, gain, weight)


def attend_kernel(q_ref, k0, k1, k2, k3, wq_ref, wkv_ref, out_ref, scores):
    queries = jnp.dot(q_ref[0], wq_ref[...], preferred_element_type=F32).astype(BF)
    queries = lax.dot_general(
        queries, wkv_ref[:, :C], (((1,), (1,)), ((), ())), preferred_element_type=F32
    )
    queries = (queries * SCALE).astype(BF)
    peak = None
    span = 2 * BLOCK
    for i, keys in enumerate((k0, k1, k2, k3)):
        s = lax.dot_general(
            queries, keys[...], (((1,), (1,)), ((), ())), preferred_element_type=F32
        )
        scores[i] = s
        high = jnp.max(s, axis=1, keepdims=True)
        peak = high if peak is None else jnp.maximum(peak, high)
    total, weighted = 0.0, 0.0
    for i, keys in enumerate((k0, k1, k2, k3)):
        e = jnp.exp2(scores[i] - peak)
        total += jnp.sum(e, axis=1, keepdims=True)
        weighted += jnp.dot(e.astype(BF), keys[...], preferred_element_type=F32)
    level = peak + jnp.log2(total)
    first = level.astype(BF).astype(F32)
    second = (level - first).astype(BF).astype(F32)
    third = level - first - second
    lane = lax.broadcasted_iota(jnp.int32, (BLOCK, 128), 1)
    out_ref[:, :C] = (weighted / total).astype(BF)
    out_ref[:, C:] = jnp.where(
        lane == 0, first, jnp.where(lane == 1, second, jnp.where(lane == 2, third, 0.0))
    ).astype(BF)


def attend_call(queries, position, keys, wq, wkv):
    return pl.pallas_call(
        attend_kernel,
        grid=(1,),
        out_shape=jax.ShapeDtypeStruct((BLOCK, C + 128), BF),
        in_specs=[pl.BlockSpec((1, BLOCK, C), lambda _: (position, 0, 0))]
        + [whole(2 * BLOCK, C)] * 4
        + [whole(C, C), whole(C, 2 * C)],
        out_specs=whole(BLOCK, C + 128),
        scratch_shapes=[pltpu.VMEM((4, BLOCK, 2 * BLOCK), F32)],
        compiler_params=PARAMS,
        name="attend",
    )(queries, *keys, wq, wkv)


def merge_kernel(p0, p1, p2, p3, wkv_ref, out_ref):
    parts = (p0, p1, p2, p3)
    levels = [jnp.sum(p[:, C:].astype(F32), axis=1, keepdims=True) for p in parts]
    peak = functools.reduce(jnp.maximum, levels)
    shares = [jnp.exp2(level - peak) for level in levels]
    mixed = sum(p[:, :C].astype(F32) * share for p, share in zip(parts, shares)) / sum(shares)
    out_ref[...] = jnp.dot(
        mixed.astype(BF), wkv_ref[:, C:], preferred_element_type=F32
    ).astype(BF)


def merge_call(parts, wkv):
    return pl.pallas_call(
        merge_kernel,
        out_shape=jax.ShapeDtypeStruct((BLOCK, C), BF),
        compiler_params=PARAMS,
        name="merge",
    )(*parts, wkv)


def final_kernel(at_ref, a0, a1, r0, r1, r2, r3, wo_ref, out_ref):
    frame, low = at_ref[0], at_ref[1]
    y0 = jnp.dot(a0[...], wo_ref[...], preferred_element_type=F32)
    y1 = jnp.dot(a1[...], wo_ref[...], preferred_element_type=F32)
    swapped = low == 1
    halves = (jnp.where(swapped, y1, y0), jnp.where(swapped, y0, y1))
    for k, r in enumerate((r0, r1, r2, r3)):
        y = halves[k // 2][(k % 2) * SLICE : (k % 2 + 1) * SLICE] + r[...]
        out_ref[frame ^ k] = y


def final_call(at, attended, residual, wo):
    vmem = pl.BlockSpec(memory_space=pltpu.VMEM)
    return pl.pallas_call(
        final_kernel,
        in_specs=[SCALAR] + [vmem] * 7,
        out_specs=vmem,
        out_shape=jax.ShapeDtypeStruct((4, SLICE, C), F32),
        compiler_params=PARAMS,
        name="final",
    )(at, *attended, *residual, wo)


def shards(
    latent, cache_first, cache_second, gain_first, conv_first, gain_second, conv_second,
    gain_attention, query_weight, keyvalue_weight, out_weight,
):
    low = lax.axis_index("yl")
    core = lax.axis_index("c")
    member = lax.axis_index("yh") * 2 + core
    index = member.astype(jnp.int32)[None]

    def sliced(v, which):
        return lax.dynamic_slice_in_dim(v, which * COLS, WIDE, axis=v.ndim - 2)

    pads = ((0, 0), (2, 2), (0, 0))
    padded = jnp.pad(latent[0], pads)
    pieces = [sliced(padded, member ^ k) for k in range(4)]
    own = [pieces[0]] + [send(pieces[k], AXES, neighbour(0, k)) for k in range(1, 4)]
    up = [send(pieces[k][ROWS - 1 :], AXES, neighbour(1, k)) for k in range(4)]
    down = [send(pieces[k][:1], AXES, neighbour(-1, k)) for k in range(4)]
    caches = jnp.pad(jnp.concatenate([cache_first, cache_second]), ((0, 0),) + pads)
    caches = sliced(caches, member)
    caches_up = send(caches[:, ROWS - 1 :], AXES, neighbour(1, 0))
    caches_down = send(caches[:, :1], AXES, neighbour(-1, 0))
    first = (caches[:2], caches_up[:2], caches_down[:2])
    second = (caches[2:], caches_up[2:], caches_down[2:])

    hidden = conv_first_call(
        index, own, up, down, first, gain_first[None], gain_second[None], conv_first
    )
    hidden_up = send(hidden[:, ROWS - 1 :], AXES, neighbour(1, 0))
    hidden_down = send(hidden[:, :1], AXES, neighbour(-1, 0))
    outs = conv_second_call(
        index, hidden, hidden_up, hidden_down, second, own, gain_attention[None], conv_second
    )
    normed, residual = outs[:4], outs[4:]

    group = ("yl", "yh", "c")
    block = jnp.concatenate([send(normed[k], group, to_plane(k)) for k in range(4)])
    other = lax.ppermute(block, "c", [(0, 1), (1, 0)])
    pair = jnp.concatenate([block, other])
    lines = ("x", "z", "c")
    keys = [
        pair,
        send(pair, lines, along(1, True)),
        send(pair, lines, along(-1, True)),
        send(pair, lines, along(2, True)),
    ]
    asked = jnp.concatenate(
        [
            lax.dynamic_slice_in_dim(k.reshape(2, BLOCK, C), (1 - core) * HALF, HALF, axis=1)
            for k in keys
        ]
    ).reshape(4, BLOCK, C)
    queries = lax.ppermute(asked, "c", [(0, 1), (1, 0)])
    residual = [residual[0]] + [
        send(residual[k], AXES, neighbour(0, k)) for k in range(1, 4)
    ]

    parts = [None] * 4
    for position, step in ((3, 2), (1, -1), (2, 1), (0, 0)):
        part = attend_call(queries, position, keys, query_weight, keyvalue_weight)
        parts[position] = send(part, lines, along(step, False)) if step else part
    attended = merge_call(parts, keyvalue_weight)
    home = ("yl", "c")
    attended = [
        send(attended[HALF:], home, to_home(0)),
        send(attended[:HALF], home, to_home(1)),
    ]
    at = jnp.stack([member, low]).astype(jnp.int32)
    out = final_call(at, attended, residual, out_weight)
    out = out.reshape(4, ROWS, COLS, C).transpose(1, 0, 2, 3).reshape(1, ROWS, 4 * COLS, C)
    return out


def solution(mesh):
    fine = Mesh(mesh.devices.reshape([SIZES[a] for a in AXES]), AXES)
    frames, rows = ("yh", "c"), ("x", "yl", "z")
    in_specs = (P(frames, rows), P(None, rows), P(None, rows)) + (P(),) * 8
    return jax.shard_map(
        shards, mesh=fine, in_specs=in_specs, out_specs=P(frames, rows), check_vma=False
    )
```

```python
import functools
import math

import jax
import jax.numpy as jnp
from jax import lax
from jax.experimental import pallas as pl
from jax.experimental.pallas import tpu as pltpu
from jax.sharding import Mesh
from jax.sharding import PartitionSpec as P

C = 384
COLS = 60
WIDE = 64
ROWS = 2
SLICE = ROWS * COLS
BLOCK = 4 * SLICE
HALF = BLOCK // 2
AXES = ("x", "yl", "z", "yh", "c")
SIZES = {"x": 4, "yl": 2, "z": 4, "yh": 2, "c": 2}
BF = jnp.bfloat16
F32 = jnp.float32
SCALE = math.log2(math.e) / math.sqrt(C)


def routes(axes, target):
    sizes = [SIZES[a] for a in axes]
    total = math.prod(sizes)
    pairs = []
    for source in range(total):
        rest, where = source, {}
        for a, n in zip(reversed(axes), reversed(sizes)):
            where[a] = rest % n
            rest //= n
        there = target(dict(where))
        if there is None:
            continue
        index = 0
        for a, n in zip(axes, sizes):
            index = index * n + there[a] % n
        pairs.append((source, index))
    return pairs


def send(value, axes, target):
    return lax.ppermute(value, axes, routes(axes, target))


def row_swap(odd):
    def target(w):
        row = (w["x"] * 2 + w["yl"]) * 4 + w["z"]
        row = ((row + 1) ^ 1) - 1 if odd else row ^ 1
        if row < 0 or row > 31:
            return None
        return {"x": row // 8, "yl": row // 4 % 2, "z": row % 4, "yh": w["yh"], "c": w["c"]}

    return target


def other(axis):
    return lambda w: {axis: 1 - w[axis]}


def to_plane(k):
    def target(w):
        frame = (w["yh"] * 2 + w["yl"]) ^ k
        return {"yh": frame // 2, "yl": frame % 2}

    return target


def line_swap(odd, key_line):
    def target(w):
        axis = "x" if (w["c"] == 0) == key_line else "z"
        w[axis] = (w[axis] + 1) % 4 ^ 1
        w[axis] = (w[axis] - 1) % 4
        return w

    def even(w):
        axis = "x" if (w["c"] == 0) == key_line else "z"
        w[axis] ^= 1
        return w

    return target if odd else even


def line_across(w):
    axis = "z" if w["c"] == 0 else "x"
    w[axis] = (w[axis] + 2) % 4
    return w


def to_home(j):
    return lambda w: {"yl": w["yl"] ^ w["c"] ^ j, "c": w["yl"]}


def norm(v, gain):
    return v * lax.rsqrt(jnp.mean(v * v, axis=-1, keepdims=True) + 1e-06) * gain


def silu(v):
    return v / (1.0 + jnp.exp(-v))


def inner_rows(frames, w_ref, acc, part_ref):
    for t in range(3):
        xs = frames[t : t + 4]
        lhs = jnp.concatenate([xs[:, 0], xs[:, 1]], axis=-1).reshape(4 * WIDE, 2 * C)
        rhs = jnp.concatenate(
            [w_ref[t, 1 - i : 3 - i, c].reshape(2 * C, C) for i in range(ROWS) for c in range(3)],
            axis=-1,
        )
        y = jnp.dot(lhs, rhs, preferred_element_type=F32)
        if t == 0:
            acc[...] = y
        else:
            acc[...] += y
    for i in range(ROWS):
        part_ref[i] = summed(acc[:, i * 3 * C : (i + 1) * 3 * C])


def outer_rows(edges, w_ref, part_ref):
    out = []
    for i in range(ROWS):
        lhs = jnp.concatenate([edges[i, t : t + 4] for t in range(3)], axis=-1)
        rhs = jnp.concatenate(
            [w_ref[:, 2 * i, c].reshape(3 * C, C) for c in range(3)], axis=-1
        )
        y = jnp.dot(lhs.reshape(4 * WIDE, 3 * C), rhs, preferred_element_type=F32)
        out.append(part_ref[i] + summed(y))
    return out


def summed(y):
    n = y.shape[0]
    return (
        pltpu.roll(y[:, :C], 1, 0) + y[:, C : 2 * C] + pltpu.roll(y[:, 2 * C :], n - 1, 0)
    )


def first_inner_kernel(at_ref, p_ref, yo_ref, co_ref, c_ref, g_ref, w_ref, part_ref, frames, acc):
    q = at_ref[0]
    frames[0:2] = c_ref[0:2]
    gain = g_ref[...].reshape(1, 1, C)
    for k, own in enumerate((p_ref[0], co_ref[0], yo_ref[0], co_ref[1])):
        frames[2 + (q ^ k)] = silu(norm(own.astype(F32), gain)).astype(BF)
    inner_rows(frames, w_ref, acc, part_ref)


def first_outer_kernel(
    at_ref, part_ref, a_ref, b_ref, ca_ref, cb_ref, g1_ref, g2_ref, w_ref,
    out_ref, out_a, out_b, edges,
):
    q, odd = at_ref[0], at_ref[1]
    for at_row, rows, cached in ((1 - odd, a_ref, ca_ref), (odd, b_ref, cb_ref)):
        edges[at_row, 0:2] = cached[0:2]
        for k in range(4):
            v = rows[k].astype(F32)
            edges[at_row, 2 + (q ^ k)] = silu(norm(v, g1_ref[...])).astype(BF)
    place = lax.broadcasted_iota(jnp.int32, (WIDE, 1), 0)
    column = place + COLS * q - 2
    valid = (column >= 0) & (column < 4 * COLS) & (place > 0) & (place < WIDE - 1)
    rows = []
    for i, y in enumerate(outer_rows(edges, w_ref, part_ref)):
        h = silu(norm(y, g2_ref[...])).reshape(4, WIDE, C)
        h = jnp.where(valid[None], h, 0.0)
        out_ref[:, i] = h.astype(BF)
        rows.append(h)
    out_a[...] = jnp.where(odd == 0, rows[1], rows[0]).astype(BF)
    out_b[...] = jnp.where(odd == 0, rows[0], rows[1]).astype(BF)


def second_inner_kernel(h_ref, c_ref, w_ref, part_ref, frames, acc):
    frames[0:2] = c_ref[2:4]
    frames[2:6] = h_ref[...]
    inner_rows(frames, w_ref, acc, part_ref)


def second_outer_kernel(
    at_ref, part_ref, a_ref, b_ref, ca_ref, cb_ref, p_ref, yo_ref, co_ref, g_ref, w_ref,
    n0, n1, n2, n3, r0, r1, r23, edges, sums, kept,
):
    q, odd, y = at_ref[0], at_ref[1], at_ref[2]
    for at_row, rows, cached in ((1 - odd, a_ref, ca_ref), (odd, b_ref, cb_ref)):
        edges[at_row, 0:2] = cached[2:4]
        edges[at_row, 2:6] = rows[...]
    for i, v in enumerate(outer_rows(edges, w_ref, part_ref)):
        sums[:, i] = v.reshape(4, WIDE, C)
    span = ROWS * WIDE
    for k, latent in enumerate((p_ref[0], co_ref[0], yo_ref[0], co_ref[1])):
        f = q ^ k
        total = (sums[f] + latent.astype(F32)).reshape(span, C)
        total = pltpu.roll(total, span - 2, 0)
        kept[f] = jnp.concatenate([total[0:COLS], total[WIDE : WIDE + COLS]], axis=0)
    for k, n_ref in enumerate((n0, n1, n2, n3)):
        n_ref[...] = norm(kept[y ^ k], g_ref[...]).astype(BF)
    r0[...] = kept[q]
    r1[...] = kept[q ^ 1]
    r23[:SLICE] = kept[q ^ 2]
    r23[SLICE:] = kept[q ^ 3]


def early_kernel(w_ref, out_ref, sems):
    copies = [pltpu.make_async_copy(w_ref.at[t], out_ref.at[t], sems.at[t]) for t in range(3)]
    for copy in copies:
        copy.start()
    for copy in copies:
        copy.wait()


SCALAR = pl.BlockSpec(memory_space=pltpu.SMEM)
FAR = pl.BlockSpec(memory_space=pl.ANY)
NEAR = pl.BlockSpec(memory_space=pltpu.VMEM)
PARAMS = pltpu.CompilerParams(vmem_limit_bytes=24 * 1024 * 1024)


def cost(flops, moved):
    return pl.CostEstimate(flops=flops, bytes_accessed=moved, transcendentals=0)


def early(weight):
    return pl.pallas_call(
        early_kernel,
        out_shape=jax.ShapeDtypeStruct(weight.shape, BF),
        in_specs=[pl.BlockSpec(memory_space=pltpu.HBM)],
        out_specs=NEAR,
        scratch_shapes=[pltpu.SemaphoreType.DMA((3,))],
        compiler_params=PARAMS,
        cost_estimate=cost(0, 2 * weight.size * 2),
        name="early",
    )(weight)


FRAMES = pltpu.VMEM((6, ROWS, WIDE, C), BF)
EDGES = pltpu.VMEM((2, 6, WIDE, C), BF)
ACC = pltpu.VMEM((4 * WIDE, ROWS * 3 * C), F32)
PART = jax.ShapeDtypeStruct((ROWS, 4 * WIDE, C), F32)
EDGE = jax.ShapeDtypeStruct((4, WIDE, C), BF)
HIDDEN = jax.ShapeDtypeStruct((4, ROWS, WIDE, C), BF)
UNIT = 2 * 4 * WIDE * 3 * C * 3 * C


def conv_call(kernel, args, scalars, out_shape, scratch, share, name):
    return pl.pallas_call(
        kernel,
        out_shape=out_shape,
        in_specs=[SCALAR] * scalars + [NEAR] * (len(args) - scalars),
        out_specs=jax.tree.map(lambda _: NEAR, out_shape),
        scratch_shapes=scratch,
        compiler_params=PARAMS,
        cost_estimate=cost(share * UNIT, 6_000_000),
        name=name,
    )(*args)


def project(raw, wq_ref, wkv_ref):
    queries = jnp.dot(raw, wq_ref[...], preferred_element_type=F32).astype(BF)
    queries = lax.dot_general(
        queries, wkv_ref[:, :C], (((1,), (1,)), ((), ())), preferred_element_type=F32
    )
    return (queries * SCALE).astype(BF)


def score(queries, keys):
    return lax.dot_general(queries, keys, (((1,), (1,)), ((), ())), preferred_element_type=F32)


def sweep(queries, buffer, cuts, before, acc, state):
    rows = queries.shape[0]
    if state is None:
        peak = jnp.full((rows, 1), -1e30, F32)
        total = jnp.zeros((rows, 1), F32)
        acc[...] = jnp.zeros((rows, C), F32)
    else:
        peak, total = state
    spans = list(zip(cuts[:-1], cuts[1:]))
    before(spans[0][1])
    scores = score(queries, buffer[spans[0][0] : spans[0][1]])
    for i, (low, high) in enumerate(spans):
        if i + 1 < len(spans):
            before(spans[i + 1][1])
            following = score(queries, buffer[spans[i + 1][0] : spans[i + 1][1]])
        risen = jnp.maximum(peak, jnp.max(scores, axis=1, keepdims=True))
        share = jnp.exp2(peak - risen)
        e = jnp.exp2(scores - risen)
        total = total * share + jnp.sum(e, axis=1, keepdims=True)
        acc[...] = acc[...] * share + jnp.dot(
            e.astype(BF), buffer[low:high], preferred_element_type=F32
        )
        peak = risen
        scores = following if i + 1 < len(spans) else None
    return peak, total


def packed(peak, total, weighted):
    lane = lax.broadcasted_iota(jnp.int32, (peak.shape[0], 128), 1)
    level = peak + jnp.log2(total)
    first = level.astype(BF).astype(F32)
    second = (level - first).astype(BF).astype(F32)
    third = level - first - second
    side = jnp.where(
        lane == 0, first, jnp.where(lane == 1, second, jnp.where(lane == 2, third, 0.0))
    )
    return jnp.concatenate([(weighted / total).astype(BF), side.astype(BF)], axis=1)


def arrivals(keys, buffer, sems):
    copies = [
        pltpu.make_async_copy(k, buffer.at[pl.ds(i * BLOCK, BLOCK)], sems.at[i])
        for i, k in enumerate(keys)
    ]
    for copy in copies:
        copy.start()
    done = [0]

    def before(row):
        while done[0] * BLOCK < row:
            copies[done[0]].wait()
            done[0] += 1

    return before


CUTS_NEAR = (0, 768, 1536, 2304, 2880)
CUTS_ALL = (0, 768, 1536, 2304, 3072, 3840)


def attend_near_kernel(qa, qb, k0, k1, k2, k3, k4, k5, wq, wkv, out, stats, ready, buffer, sems):
    before = arrivals((k0, k1, k2, k3, k4, k5), buffer, sems)
    queries = project(jnp.concatenate([qa[...], qb[...]], axis=0), wq, wkv)
    ready[...] = queries
    peak, total = sweep(queries, buffer, CUTS_NEAR, before, out, None)
    lane = lax.broadcasted_iota(jnp.int32, (2 * BLOCK, 128), 1)
    stats[...] = jnp.where(lane == 0, peak, total)


def attend_far_kernel(ready, weighted, stats, k6, k7, wq, wkv, out_a, out_b, buffer, sems, acc):
    before = arrivals((k6, k7), buffer, sems)
    acc[...] = weighted[...]
    state = (stats[:, 0:1], stats[:, 1:2])
    peak, total = sweep(ready[...], buffer, (0, 2 * BLOCK), before, acc, state)
    result = packed(peak, total, acc[...])
    out_a[...] = result[:BLOCK]
    out_b[...] = result[BLOCK:]


def attend_all_kernel(q, k0, k1, k2, k3, k4, k5, k6, k7, wq, wkv, out, buffer, sems, acc):
    before = arrivals((k0, k1, k2, k3, k4, k5, k6, k7), buffer, sems)
    queries = project(q[...], wq, wkv)
    peak, total = sweep(queries, buffer, CUTS_ALL, before, acc, None)
    out[...] = packed(peak, total, acc[...])


def attend(kernel, first, keys, weights, out_shape, scratch, flops, name):
    n = len(keys)
    return pl.pallas_call(
        kernel,
        out_shape=out_shape,
        in_specs=[NEAR] * len(first) + [FAR] * n + [NEAR] * 2,
        out_specs=[NEAR] * len(out_shape),
        scratch_shapes=[pltpu.VMEM((n * BLOCK, C), BF), pltpu.SemaphoreType.DMA((n,))] + scratch,
        compiler_params=PARAMS,
        cost_estimate=cost(2 * flops, n * 2 * BLOCK * C),
        name=name,
    )(*first, *keys, *weights)


def merge_kernel(at_ref, p0, p1, p2, p3, wkv_ref, out_a, out_b):
    parts = (p0, p1, p2, p3)
    levels = [jnp.sum(p[:, C:].astype(F32), axis=1, keepdims=True) for p in parts]
    peak = functools.reduce(jnp.maximum, levels)
    shares = [jnp.exp2(level - peak) for level in levels]
    mixed = sum(p[:, :C].astype(F32) * share for p, share in zip(parts, shares)) / sum(shares)
    y = jnp.dot(mixed.astype(BF), wkv_ref[:, C:], preferred_element_type=F32)
    even = jnp.concatenate([y[:SLICE], y[2 * SLICE : 3 * SLICE]], axis=0)
    odd = jnp.concatenate([y[SLICE : 2 * SLICE], y[3 * SLICE :]], axis=0)
    core = at_ref[3]
    out_a[...] = jnp.where(core == 0, even, odd).astype(BF)
    out_b[...] = jnp.where(core == 0, odd, even).astype(BF)


def merge_call(at, parts, wkv):
    return pl.pallas_call(
        merge_kernel,
        in_specs=[SCALAR] + [NEAR] * 5,
        out_specs=[NEAR] * 2,
        out_shape=[jax.ShapeDtypeStruct((HALF, C), BF)] * 2,
        compiler_params=PARAMS,
        name="merge",
    )(at, *parts, wkv)


def final_kernel(at_ref, a_ref, b_ref, r0, ry, rc, wo_ref, out_ref, parts):
    frame, low = at_ref[0], at_ref[4]
    ya = jnp.dot(a_ref[...], wo_ref[...], preferred_element_type=F32)
    yb = jnp.dot(b_ref[...], wo_ref[...], preferred_element_type=F32)
    even, odd = jnp.where(low == 0, yb, ya), jnp.where(low == 0, ya, yb)
    parts[0] = even[:SLICE] + r0[...]
    parts[1] = odd[:SLICE] + rc[:SLICE]
    parts[2] = even[SLICE:] + ry[:SLICE]
    parts[3] = odd[SLICE:] + rc[SLICE:]
    for q in range(4):
        part = parts[frame ^ q]
        out_ref[0, 0, q * COLS : (q + 1) * COLS] = part[:COLS]
        out_ref[0, 1, q * COLS : (q + 1) * COLS] = part[COLS:]


def final_call(at, a, b, r0, ry, rc, wo):
    return pl.pallas_call(
        final_kernel,
        in_specs=[SCALAR] + [NEAR] * 6,
        out_specs=NEAR,
        out_shape=jax.ShapeDtypeStruct((1, ROWS, 4 * COLS, C), F32),
        scratch_shapes=[pltpu.VMEM((4, SLICE, C), F32)],
        compiler_params=PARAMS,
        name="final",
    )(at, a, b, r0, ry, rc, wo)


def shards(
    latent, cache_first, cache_second, gain_first, conv_first, gain_second, conv_second,
    gain_attention, query_weight, keyvalue_weight, out_weight,
):
    low, high, core = (lax.axis_index(a) for a in ("yl", "yh", "c"))
    member = high * 2 + core
    odd = lax.axis_index("z") % 2
    at = jnp.stack([member, odd, high * 2 + low, core, low]).astype(jnp.int32)

    def sliced(v, which):
        return lax.dynamic_slice_in_dim(v, which * COLS, WIDE, axis=v.ndim - 2)

    def row(v, which):
        return lax.dynamic_index_in_dim(v, which, axis=1, keepdims=False)

    pads = ((0, 0), (2, 2), (0, 0))
    padded = jnp.pad(latent[0], pads)
    pieces = jnp.stack([sliced(padded, member ^ k) for k in range(4)])
    yo = send(pieces[2:], ("yh",), other("yh"))
    caches = jnp.pad(jnp.concatenate([cache_first, cache_second]), ((0, 0),) + pads)
    caches = sliced(caches, member)
    ca = send(row(caches, 1 - odd), AXES, row_swap(False))
    cb = send(row(caches, odd), AXES, row_swap(True))
    weight1, weight2 = early(conv_first), early(conv_second)
    co = send(jnp.stack([pieces[1], yo[1]]), ("c",), other("c"))

    edge = jnp.stack([pieces[0], co[0], yo[0], co[1]])
    a = send(row(edge, 1 - odd), AXES, row_swap(False))
    b = send(row(edge, odd), AXES, row_swap(True))
    gain1, gain2, gain3 = gain_first[None], gain_second[None], gain_attention[None]
    part = conv_call(
        first_inner_kernel, (at, pieces, yo, co, caches, gain1, weight1), 1, PART,
        [FRAMES, ACC], 6, "first_inner",
    )
    hidden, ha, hb = conv_call(
        first_outer_kernel, (at, part, a, b, ca, cb, gain1, gain2, weight1), 1,
        [HIDDEN, EDGE, EDGE], [EDGES], 2, "first_outer",
    )
    ha = send(ha, AXES, row_swap(False))
    hb = send(hb, AXES, row_swap(True))
    part = conv_call(
        second_inner_kernel, (hidden, caches, weight2), 0, PART, [FRAMES, ACC], 6,
        "second_inner",
    )
    slice_of = lambda n, kind: jax.ShapeDtypeStruct((n * SLICE, C), kind)
    n0, n1, n2, n3, r0, r1, r23 = conv_call(
        second_outer_kernel,
        (at, part, ha, hb, ca, cb, pieces, yo, co, gain3, weight2), 1,
        [slice_of(1, BF)] * 4 + [slice_of(1, F32)] * 2 + [slice_of(2, F32)],
        [EDGES, pltpu.VMEM((4, ROWS, WIDE, C), F32), pltpu.VMEM((4, SLICE, C), F32)], 2,
        "second_outer",
    )

    group = ("yl", "yh")
    block = jnp.concatenate([n0] + [send(n, group, to_plane(k + 1)) for k, n in enumerate((n1, n2, n3))])
    lines = ("x", "z", "c")
    cross = lambda v: send(v, ("c",), other("c"))
    keyed = lambda v, turn: send(v, lines, line_swap(turn, True))
    asked = lambda v, turn: send(v, lines, line_swap(turn, False))
    p0, p1 = block, cross(block)
    a0, b0 = keyed(p0, False), keyed(p0, True)
    a1, b1 = keyed(p1, False), keyed(p1, True)
    ab, ba = keyed(a0, True), keyed(b1, False)
    qa, qb = cross(a0), cross(b0)
    weights = (query_weight, keyvalue_weight)

    near_keys = [p0, p1, a0, b1, a1, b0]
    every = near_keys + [ab, ba]
    unit = 4 * BLOCK * BLOCK * C
    wide = jax.ShapeDtypeStruct((BLOCK, C + 128), BF)
    weighted, stats, ready = attend(
        attend_near_kernel, [qa, qb], near_keys, weights,
        [
            jax.ShapeDtypeStruct((2 * BLOCK, C), F32),
            jax.ShapeDtypeStruct((2 * BLOCK, 128), F32),
            jax.ShapeDtypeStruct((2 * BLOCK, C), BF),
        ],
        [], 12 * unit, "attend_near",
    )
    after = lambda v, mark: lax.optimization_barrier((v, mark))[0]
    qo = cross(after(ab, stats))
    ry = send(after(r23, stats), ("yh",), other("yh"))
    sa, sb = attend(
        attend_far_kernel, [ready, weighted, stats], [ab, ba], weights, [wide] * 2,
        [pltpu.VMEM((2 * BLOCK, C), F32)], 4 * unit, "attend_far",
    )
    (to,) = attend(
        attend_all_kernel, [after(qo, sa)], every, weights, [wide],
        [pltpu.VMEM((BLOCK, C), F32)], 8 * unit, "attend_across",
    )
    sa, sb = asked(sa, False), asked(sb, True)
    (own,) = attend(
        attend_all_kernel, [after(p1, to)], every, weights, [wide],
        [pltpu.VMEM((BLOCK, C), F32)], 8 * unit, "attend_own",
    )
    rc = cross(jnp.concatenate([r1, after(ry, sa)[SLICE:]]))
    to = send(to, lines, line_across)
    to_a, to_b = merge_call(at, (own, sa, sb, to), keyvalue_weight)
    home = ("yl", "c")
    to_a, to_b = send(to_a, home, to_home(0)), send(to_b, home, to_home(1))
    return final_call(at, to_a, to_b, r0, ry, rc, out_weight)


def solution(mesh):
    fine = Mesh(mesh.devices.reshape([SIZES[a] for a in AXES]), AXES)
    frames, rows = ("yh", "c"), ("x", "yl", "z")
    in_specs = (P(frames, rows), P(None, rows), P(None, rows)) + (P(),) * 8
    return jax.shard_map(
        shards, mesh=fine, in_specs=in_specs, out_specs=P(frames, rows), check_vma=False
    )
```

```python
import functools
import math

import jax
import jax.numpy as jnp
from jax import lax
from jax.experimental import pallas as pl
from jax.experimental.pallas import tpu as pltpu
from jax.sharding import Mesh
from jax.sharding import PartitionSpec as P

C = 384
COLS = 60
WIDE = 64
ROWS = 2
SLICE = ROWS * COLS
BLOCK = 4 * SLICE
HALF = BLOCK // 2
AXES = ("x", "yl", "z", "yh", "c")
SIZES = {"x": 4, "yl": 2, "z": 4, "yh": 2, "c": 2}
BF = jnp.bfloat16
F32 = jnp.float32
SCALE = math.log2(math.e) / math.sqrt(C)


def routes(axes, target):
    sizes = [SIZES[a] for a in axes]
    total = math.prod(sizes)
    pairs = []
    for source in range(total):
        rest, where = source, {}
        for a, n in zip(reversed(axes), reversed(sizes)):
            where[a] = rest % n
            rest //= n
        there = target(dict(where))
        if there is None:
            continue
        index = 0
        for a, n in zip(axes, sizes):
            index = index * n + there[a] % n
        pairs.append((source, index))
    return pairs


def send(value, axes, target):
    return lax.ppermute(value, axes, routes(axes, target))


def row_swap(odd):
    def target(w):
        row = (w["x"] * 2 + w["yl"]) * 4 + w["z"]
        row = ((row + 1) ^ 1) - 1 if odd else row ^ 1
        if row < 0 or row > 31:
            return None
        return {"x": row // 8, "yl": row // 4 % 2, "z": row % 4, "yh": w["yh"], "c": w["c"]}

    return target


def other(axis):
    return lambda w: {axis: 1 - w[axis]}


def to_plane(k):
    def target(w):
        frame = (w["yh"] * 2 + w["yl"]) ^ k
        return {"yh": frame // 2, "yl": frame % 2}

    return target


def line_swap(odd, key_line):
    def target(w):
        axis = "x" if (w["c"] == 0) == key_line else "z"
        w[axis] = (w[axis] + 1) % 4 ^ 1
        w[axis] = (w[axis] - 1) % 4
        return w

    def even(w):
        axis = "x" if (w["c"] == 0) == key_line else "z"
        w[axis] ^= 1
        return w

    return target if odd else even


def line_across(w):
    axis = "z" if w["c"] == 0 else "x"
    w[axis] = (w[axis] + 2) % 4
    return w


def to_home(j):
    return lambda w: {"yl": w["yl"] ^ w["c"] ^ j, "c": w["yl"]}


def norm(v, gain):
    return v * lax.rsqrt(jnp.mean(v * v, axis=-1, keepdims=True) + 1e-06) * gain


def silu(v):
    return v / (1.0 + jnp.exp(-v))


def inner_rows(frames, w_ref, acc, part_ref):
    for t in range(3):
        xs = frames[t : t + 4]
        lhs = jnp.concatenate([xs[:, 0], xs[:, 1]], axis=-1).reshape(4 * WIDE, 2 * C)
        rhs = jnp.concatenate(
            [w_ref[t, 1 - i : 3 - i, c].reshape(2 * C, C) for i in range(ROWS) for c in range(3)],
            axis=-1,
        )
        y = jnp.dot(lhs, rhs, preferred_element_type=F32)
        if t == 0:
            acc[...] = y
        else:
            acc[...] += y
    for i in range(ROWS):
        part_ref[i] = summed(acc[:, i * 3 * C : (i + 1) * 3 * C])


def outer_rows(edges, w_ref, part_ref):
    out = []
    for i in range(ROWS):
        lhs = jnp.concatenate([edges[i, t : t + 4] for t in range(3)], axis=-1)
        rhs = jnp.concatenate(
            [w_ref[:, 2 * i, c].reshape(3 * C, C) for c in range(3)], axis=-1
        )
        y = jnp.dot(lhs.reshape(4 * WIDE, 3 * C), rhs, preferred_element_type=F32)
        out.append(part_ref[i] + summed(y))
    return out


def summed(y):
    n = y.shape[0]
    return (
        pltpu.roll(y[:, :C], 1, 0) + y[:, C : 2 * C] + pltpu.roll(y[:, 2 * C :], n - 1, 0)
    )


def windows(v):
    edge = jnp.zeros((v.shape[0], 2, C), F32)
    v = jnp.concatenate([edge, v.astype(F32), edge], axis=1)
    return [v[:, q * COLS : q * COLS + WIDE].astype(BF) for q in range(4)]


def pieces_kernel(at_ref, v_ref, own_ref, near_ref, far_ref, held):
    q = at_ref[0]
    for i, window in enumerate(windows(v_ref[0])):
        held[i] = window
    own_ref[...] = held[q]
    near_ref[...] = held[q ^ 1]
    far_ref[0] = held[q ^ 2]
    far_ref[1] = held[q ^ 3]


def caches_kernel(at_ref, first_ref, second_ref, out_ref, held):
    for n, ref in enumerate((first_ref, second_ref)):
        for f in range(2):
            for i, window in enumerate(windows(ref[f])):
                held[i] = window
            out_ref[2 * n + f] = held[at_ref[0]]


def relay_kernel(near_ref, yo_ref, out_ref):
    out_ref[0] = near_ref[...]
    out_ref[1] = yo_ref[1]


def edges_kernel(at_ref, own_ref, yo_ref, co_ref, c_ref, a_ref, b_ref):
    odd = at_ref[1]
    refs = (own_ref, co_ref.at[0], yo_ref.at[0], co_ref.at[1], c_ref.at[0], c_ref.at[1])
    for k, ref in enumerate(refs):
        top, bottom = ref[0], ref[1]
        a_ref[k] = jnp.where(odd == 0, bottom, top)
        b_ref[k] = jnp.where(odd == 0, top, bottom)


def first_inner_kernel(at_ref, p_ref, yo_ref, co_ref, c_ref, g_ref, w_ref, part_ref, frames, acc):
    q = at_ref[0]
    frames[0:2] = c_ref[0:2]
    gain = g_ref[...]
    for k, own in enumerate((p_ref[...], co_ref[0], yo_ref[0], co_ref[1])):
        frames[2 + (q ^ k)] = silu(norm(own.astype(F32), gain)).astype(BF)
    inner_rows(frames, w_ref, acc, part_ref)


def first_outer_kernel(
    at_ref, part_ref, a_ref, b_ref, c_ref, g1_ref, g2_ref, w_ref,
    out_ref, out_a, out_b, edges,
):
    q, odd = at_ref[0], at_ref[1]
    for at_row, rows in ((1 - odd, a_ref), (odd, b_ref)):
        edges[at_row, 0:2] = rows[4:6]
        for k in range(4):
            v = rows[k].astype(F32)
            edges[at_row, 2 + (q ^ k)] = silu(norm(v, g1_ref[...])).astype(BF)
    place = lax.broadcasted_iota(jnp.int32, (WIDE, 1), 0)
    column = place + COLS * q - 2
    valid = (column >= 0) & (column < 4 * COLS) & (place > 0) & (place < WIDE - 1)
    rows = []
    for i, y in enumerate(outer_rows(edges, w_ref, part_ref)):
        h = silu(norm(y, g2_ref[...])).reshape(4, WIDE, C)
        h = jnp.where(valid[None], h, 0.0)
        out_ref[:, i] = h.astype(BF)
        rows.append(h)
    out_a[0:4] = jnp.where(odd == 0, rows[1], rows[0]).astype(BF)
    out_b[0:4] = jnp.where(odd == 0, rows[0], rows[1]).astype(BF)
    for f in range(2):
        out_a[4 + f] = jnp.where(odd == 0, c_ref[2 + f, 1], c_ref[2 + f, 0])
        out_b[4 + f] = jnp.where(odd == 0, c_ref[2 + f, 0], c_ref[2 + f, 1])


def second_inner_kernel(h_ref, c_ref, w_ref, part_ref, frames, acc):
    frames[0:2] = c_ref[2:4]
    frames[2:6] = h_ref[...]
    inner_rows(frames, w_ref, acc, part_ref)


def second_outer_kernel(
    at_ref, part_ref, a_ref, b_ref, p_ref, yo_ref, co_ref, g_ref, w_ref,
    n0, n1, n2, n3, r0, r1, r23, edges, sums, kept,
):
    q, odd, y = at_ref[0], at_ref[1], at_ref[2]
    for at_row, rows in ((1 - odd, a_ref), (odd, b_ref)):
        edges[at_row, 0:2] = rows[4:6]
        edges[at_row, 2:6] = rows[0:4]
    for i, v in enumerate(outer_rows(edges, w_ref, part_ref)):
        sums[:, i] = v.reshape(4, WIDE, C)
    span = ROWS * WIDE
    for k, latent in enumerate((p_ref[...], co_ref[0], yo_ref[0], co_ref[1])):
        f = q ^ k
        total = (sums[f] + latent.astype(F32)).reshape(span, C)
        total = pltpu.roll(total, span - 2, 0)
        kept[f] = jnp.concatenate([total[0:COLS], total[WIDE : WIDE + COLS]], axis=0)
    for k, n_ref in enumerate((n0, n1, n2, n3)):
        n_ref[...] = norm(kept[y ^ k], g_ref[...]).astype(BF)
    r0[...] = kept[q]
    r1[...] = kept[q ^ 1]
    r23[:SLICE] = kept[q ^ 2]
    r23[SLICE:] = kept[q ^ 3]


SCALAR = pl.BlockSpec(memory_space=pltpu.SMEM)
FAR = pl.BlockSpec(memory_space=pl.ANY)
NEAR = pl.BlockSpec(memory_space=pltpu.VMEM)
PARAMS = pltpu.CompilerParams(vmem_limit_bytes=24 * 1024 * 1024)


def cost(flops, moved):
    return pl.CostEstimate(flops=flops, bytes_accessed=moved, transcendentals=0)


FRAMES = pltpu.VMEM((6, ROWS, WIDE, C), BF)
EDGES = pltpu.VMEM((2, 6, WIDE, C), BF)
ACC = pltpu.VMEM((4 * WIDE, ROWS * 3 * C), F32)
PART = jax.ShapeDtypeStruct((ROWS, 4 * WIDE, C), F32)
EDGE = jax.ShapeDtypeStruct((6, WIDE, C), BF)
HIDDEN = jax.ShapeDtypeStruct((4, ROWS, WIDE, C), BF)
UNIT = 2 * 4 * WIDE * 3 * C * 3 * C


def conv_call(kernel, args, scalars, out_shape, scratch, share, name):
    return pl.pallas_call(
        kernel,
        out_shape=out_shape,
        in_specs=[SCALAR] * scalars + [NEAR] * (len(args) - scalars),
        out_specs=jax.tree.map(lambda _: NEAR, out_shape),
        scratch_shapes=scratch,
        compiler_params=PARAMS,
        cost_estimate=cost(share * UNIT, 6_000_000),
        name=name,
    )(*args)


def project(raw, wq_ref, wkv_ref):
    queries = jnp.dot(raw, wq_ref[...], preferred_element_type=F32).astype(BF)
    queries = lax.dot_general(
        queries, wkv_ref[:, :C], (((1,), (1,)), ((), ())), preferred_element_type=F32
    )
    return (queries * SCALE).astype(BF)


def score(queries, keys):
    return lax.dot_general(queries, keys, (((1,), (1,)), ((), ())), preferred_element_type=F32)


def sweep(queries, buffer, cuts, before, acc, state):
    rows = queries.shape[0]
    if state is None:
        peak = jnp.full((rows, 1), -1e30, F32)
        total = jnp.zeros((rows, 1), F32)
        acc[...] = jnp.zeros((rows, C), F32)
    else:
        peak, total = state
    spans = list(zip(cuts[:-1], cuts[1:]))
    before(spans[0][1])
    scores = score(queries, buffer[spans[0][0] : spans[0][1]])
    for i, (low, high) in enumerate(spans):
        if i + 1 < len(spans):
            before(spans[i + 1][1])
            following = score(queries, buffer[spans[i + 1][0] : spans[i + 1][1]])
        risen = jnp.maximum(peak, jnp.max(scores, axis=1, keepdims=True))
        share = jnp.exp2(peak - risen)
        e = jnp.exp2(scores - risen)
        total = total * share + jnp.sum(e, axis=1, keepdims=True)
        acc[...] = acc[...] * share + jnp.dot(
            e.astype(BF), buffer[low:high], preferred_element_type=F32
        )
        peak = risen
        scores = following if i + 1 < len(spans) else None
    return peak, total


def packed(peak, total, weighted):
    lane = lax.broadcasted_iota(jnp.int32, (peak.shape[0], 128), 1)
    level = peak + jnp.log2(total)
    first = level.astype(BF).astype(F32)
    second = (level - first).astype(BF).astype(F32)
    third = level - first - second
    side = jnp.where(
        lane == 0, first, jnp.where(lane == 1, second, jnp.where(lane == 2, third, 0.0))
    )
    return jnp.concatenate([(weighted / total).astype(BF), side.astype(BF)], axis=1)


def arrivals(keys, buffer, sems):
    copies = [
        pltpu.make_async_copy(k, buffer.at[pl.ds(i * BLOCK, BLOCK)], sems.at[i])
        for i, k in enumerate(keys)
    ]
    for copy in copies:
        copy.start()
    done = [0]

    def before(row):
        while done[0] * BLOCK < row:
            copies[done[0]].wait()
            done[0] += 1

    return before


CUTS_HALF = (0, 768, 1536, 1920)
CUTS_ALL = (0, 768, 1536, 2304, 3072, 3840)


def attend_near_kernel(qa, qb, k0, k1, k2, k3, wq, wkv, out, stats, ready, buffer, sems):
    before = arrivals((k0, k1, k2, k3), buffer, sems)
    queries = project(jnp.concatenate([qa[...], qb[...]], axis=0), wq, wkv)
    ready[...] = queries
    peak, total = sweep(queries, buffer, CUTS_HALF, before, out, None)
    lane = lax.broadcasted_iota(jnp.int32, (2 * BLOCK, 128), 1)
    stats[...] = jnp.where(lane == 0, peak, total)


def attend_far_kernel(
    ready, weighted, stats, k0, k1, k2, k3, wq, wkv, out_a, out_b, buffer, sems, acc
):
    before = arrivals((k0, k1, k2, k3), buffer, sems)
    acc[...] = weighted[...]
    state = (stats[:, 0:1], stats[:, 1:2])
    peak, total = sweep(ready[...], buffer, CUTS_HALF, before, acc, state)
    result = packed(peak, total, acc[...])
    out_a[...] = result[:BLOCK]
    out_b[...] = result[BLOCK:]


def attend_all_kernel(q, k0, k1, k2, k3, k4, k5, k6, k7, wq, wkv, out, buffer, sems, acc):
    before = arrivals((k0, k1, k2, k3, k4, k5, k6, k7), buffer, sems)
    queries = project(q[...], wq, wkv)
    peak, total = sweep(queries, buffer, CUTS_ALL, before, acc, None)
    out[...] = packed(peak, total, acc[...])


def attend(kernel, first, keys, weights, out_shape, scratch, flops, name):
    n = len(keys)
    return pl.pallas_call(
        kernel,
        out_shape=out_shape,
        in_specs=[NEAR] * len(first) + [FAR] * n + [NEAR] * 2,
        out_specs=[NEAR] * len(out_shape),
        scratch_shapes=[pltpu.VMEM((n * BLOCK, C), BF), pltpu.SemaphoreType.DMA((n,))] + scratch,
        compiler_params=PARAMS,
        cost_estimate=cost(2 * flops, n * 2 * BLOCK * C),
        name=name,
    )(*first, *keys, *weights)


def merge_kernel(at_ref, p0, p1, p2, p3, wkv_ref, out_a, out_b):
    parts = (p0, p1, p2, p3)
    levels = [jnp.sum(p[:, C:].astype(F32), axis=1, keepdims=True) for p in parts]
    peak = functools.reduce(jnp.maximum, levels)
    shares = [jnp.exp2(level - peak) for level in levels]
    mixed = sum(p[:, :C].astype(F32) * share for p, share in zip(parts, shares)) / sum(shares)
    y = jnp.dot(mixed.astype(BF), wkv_ref[:, C:], preferred_element_type=F32)
    even = jnp.concatenate([y[:SLICE], y[2 * SLICE : 3 * SLICE]], axis=0)
    odd = jnp.concatenate([y[SLICE : 2 * SLICE], y[3 * SLICE :]], axis=0)
    core = at_ref[3]
    out_a[...] = jnp.where(core == 0, even, odd).astype(BF)
    out_b[...] = jnp.where(core == 0, odd, even).astype(BF)


def merge_call(at, parts, wkv):
    return pl.pallas_call(
        merge_kernel,
        in_specs=[SCALAR] + [NEAR] * 5,
        out_specs=[NEAR] * 2,
        out_shape=[jax.ShapeDtypeStruct((HALF, C), BF)] * 2,
        compiler_params=PARAMS,
        name="merge",
    )(at, *parts, wkv)


def final_kernel(at_ref, a_ref, b_ref, r0, ry, rc, wo_ref, out_ref, parts):
    frame, low = at_ref[0], at_ref[4]
    ya = jnp.dot(a_ref[...], wo_ref[...], preferred_element_type=F32)
    yb = jnp.dot(b_ref[...], wo_ref[...], preferred_element_type=F32)
    even, odd = jnp.where(low == 0, ya, yb), jnp.where(low == 0, yb, ya)
    parts[0] = even[:SLICE] + r0[...]
    parts[1] = odd[:SLICE] + rc[:SLICE]
    parts[2] = even[SLICE:] + ry[:SLICE]
    parts[3] = odd[SLICE:] + rc[SLICE:]
    for q in range(4):
        part = parts[frame ^ q]
        out_ref[0, 0, q * COLS : (q + 1) * COLS] = part[:COLS]
        out_ref[0, 1, q * COLS : (q + 1) * COLS] = part[COLS:]


def final_call(at, a, b, r0, ry, rc, wo):
    return pl.pallas_call(
        final_kernel,
        in_specs=[SCALAR] + [NEAR] * 6,
        out_specs=NEAR,
        out_shape=jax.ShapeDtypeStruct((1, ROWS, 4 * COLS, C), F32),
        scratch_shapes=[pltpu.VMEM((4, SLICE, C), F32)],
        compiler_params=PARAMS,
        name="final",
    )(at, a, b, r0, ry, rc, wo)


def shards(
    latent, cache_first, cache_second, gain_first, conv_first, gain_second, conv_second,
    gain_attention, query_weight, keyvalue_weight, out_weight,
):
    low, high, core = (lax.axis_index(a) for a in ("yl", "yh", "c"))
    member = high * 2 + core
    odd = lax.axis_index("z") % 2
    at = jnp.stack([member, odd, high * 2 + low, core, low]).astype(jnp.int32)

    both = jax.ShapeDtypeStruct((ROWS, WIDE, C), BF)
    two = jax.ShapeDtypeStruct((2, ROWS, WIDE, C), BF)
    held = [pltpu.VMEM((4, ROWS, WIDE, C), BF)]
    pieces, near, far = conv_call(
        pieces_kernel, (at, latent), 1, [both, both, two], held, 0, "pieces"
    )
    yo = send(far, ("yh",), other("yh"))
    caches = conv_call(
        caches_kernel, (at, cache_first, cache_second), 1, HIDDEN, held, 0, "caches"
    )
    near, caches = lax.optimization_barrier((near, caches))
    co = conv_call(relay_kernel, (near, yo), 0, two, [], 0, "relay")
    co = send(co, ("c",), other("c"))

    a, b = conv_call(edges_kernel, (at, pieces, yo, co, caches), 1, [EDGE, EDGE], [], 0, "edges")
    a = send(a, AXES, row_swap(False))
    b = send(b, AXES, row_swap(True))
    gain1, gain2, gain3 = gain_first, gain_second, gain_attention
    part = conv_call(
        first_inner_kernel, (at, pieces, yo, co, caches, gain1, conv_first), 1, PART,
        [FRAMES, ACC], 6, "first_inner",
    )
    hidden, ha, hb = conv_call(
        first_outer_kernel, (at, part, a, b, caches, gain1, gain2, conv_first), 1,
        [HIDDEN, EDGE, EDGE], [EDGES], 2, "first_outer",
    )
    ha = send(ha, AXES, row_swap(False))
    hb = send(hb, AXES, row_swap(True))
    part = conv_call(
        second_inner_kernel, (hidden, caches, conv_second), 0, PART, [FRAMES, ACC], 6,
        "second_inner",
    )
    slice_of = lambda n, kind: jax.ShapeDtypeStruct((n * SLICE, C), kind)
    n0, n1, n2, n3, r0, r1, r23 = conv_call(
        second_outer_kernel,
        (at, part, ha, hb, pieces, yo, co, gain3, conv_second), 1,
        [slice_of(1, BF)] * 4 + [slice_of(1, F32)] * 2 + [slice_of(2, F32)],
        [EDGES, pltpu.VMEM((4, ROWS, WIDE, C), F32), pltpu.VMEM((4, SLICE, C), F32)], 2,
        "second_outer",
    )

    group = ("yl", "yh")
    block = jnp.concatenate([n0] + [send(n, group, to_plane(k + 1)) for k, n in enumerate((n1, n2, n3))])
    lines = ("x", "z", "c")
    cross = lambda v: send(v, ("c",), other("c"))
    keyed = lambda v, turn: send(v, lines, line_swap(turn, True))
    asked = lambda v, turn: send(v, lines, line_swap(turn, False))
    p0 = block
    a0, b0 = keyed(p0, False), keyed(p0, True)
    qa, qb = asked(p0, False), asked(p0, True)
    p1 = cross(p0)
    ab, qo = keyed(a0, True), asked(qa, True)
    a1, b1 = cross(qa), cross(qb)
    weights = (query_weight, keyvalue_weight)

    near_keys = [p0, p1, a0, b0]
    unit = 4 * BLOCK * BLOCK * C
    wide = jax.ShapeDtypeStruct((BLOCK, C + 128), BF)
    weighted, stats, ready = attend(
        attend_near_kernel, [qa, qb], near_keys, weights,
        [
            jax.ShapeDtypeStruct((2 * BLOCK, C), F32),
            jax.ShapeDtypeStruct((2 * BLOCK, 128), F32),
            jax.ShapeDtypeStruct((2 * BLOCK, C), BF),
        ],
        [], 8 * unit, "attend_near",
    )
    after = lambda v, mark: lax.optimization_barrier((v, mark))[0]
    ba = cross(after(qo, stats))
    ry = send(after(r23, stats), ("yh",), other("yh"))
    far_keys = [a1, b1, ab, ba]
    every = near_keys + far_keys
    sa, sb = attend(
        attend_far_kernel, [ready, weighted, stats], far_keys, weights, [wide] * 2,
        [pltpu.VMEM((2 * BLOCK, C), F32)], 8 * unit, "attend_far",
    )
    (to,) = attend(
        attend_all_kernel, [after(qo, sa)], every, weights, [wide],
        [pltpu.VMEM((BLOCK, C), F32)], 8 * unit, "attend_across",
    )
    sa, sb = asked(sa, False), asked(sb, True)
    (own,) = attend(
        attend_all_kernel, [after(p0, to)], every, weights, [wide],
        [pltpu.VMEM((BLOCK, C), F32)], 8 * unit, "attend_own",
    )
    rc = cross(jnp.concatenate([r1, after(ry, sa)[SLICE:]]))
    to = send(to, lines, line_across)
    to_a, to_b = merge_call(at, (own, sa, sb, to), keyvalue_weight)
    home = ("yl", "c")
    to_a, to_b = send(to_a, home, to_home(0)), send(to_b, home, to_home(1))
    return final_call(at, to_a, to_b, r0, ry, rc, out_weight)


def solution(mesh):
    fine = Mesh(mesh.devices.reshape([SIZES[a] for a in AXES]), AXES)
    frames, rows = ("yh", "c"), ("x", "yl", "z")
    in_specs = (P(frames, rows), P(None, rows), P(None, rows)) + (P(),) * 8
    return jax.shard_map(
        shards, mesh=fine, in_specs=in_specs, out_specs=P(frames, rows), check_vma=False
    )
```

```python
import functools
import math

import jax
import jax.numpy as jnp
from jax import lax
from jax.experimental import pallas as pl
from jax.experimental.pallas import tpu as pltpu
from jax.sharding import Mesh
from jax.sharding import PartitionSpec as P

C = 384
COLS = 60
WIDE = 64
ROWS = 2
SLICE = ROWS * COLS
BLOCK = 4 * SLICE
HALF = BLOCK // 2
AXES = ("x", "yl", "z", "yh", "c")
SIZES = {"x": 4, "yl": 2, "z": 4, "yh": 2, "c": 2}
BF = jnp.bfloat16
F32 = jnp.float32
SCALE = math.log2(math.e) / math.sqrt(C)


def routes(axes, target):
    sizes = [SIZES[a] for a in axes]
    total = math.prod(sizes)
    pairs = []
    for source in range(total):
        rest, where = source, {}
        for a, n in zip(reversed(axes), reversed(sizes)):
            where[a] = rest % n
            rest //= n
        there = target(dict(where))
        if there is None:
            continue
        index = 0
        for a, n in zip(axes, sizes):
            index = index * n + there[a] % n
        pairs.append((source, index))
    return pairs


def send(value, axes, target):
    return lax.ppermute(value, axes, routes(axes, target))


def row_swap(odd):
    def target(w):
        row = (w["x"] * 2 + w["yl"]) * 4 + w["z"]
        row = ((row + 1) ^ 1) - 1 if odd else row ^ 1
        if row < 0 or row > 31:
            return None
        return {"x": row // 8, "yl": row // 4 % 2, "z": row % 4, "yh": w["yh"], "c": w["c"]}

    return target


def other(axis):
    return lambda w: {axis: 1 - w[axis]}


def to_plane(k):
    def target(w):
        frame = (w["yh"] * 2 + w["yl"]) ^ k
        return {"yh": frame // 2, "yl": frame % 2}

    return target


def line_swap(odd, key_line):
    def target(w):
        axis = "x" if (w["c"] == 0) == key_line else "z"
        w[axis] = (w[axis] + 1) % 4 ^ 1
        w[axis] = (w[axis] - 1) % 4
        return w

    def even(w):
        axis = "x" if (w["c"] == 0) == key_line else "z"
        w[axis] ^= 1
        return w

    return target if odd else even


def line_across(w):
    axis = "z" if w["c"] == 0 else "x"
    w[axis] = (w[axis] + 2) % 4
    return w


def to_home(j):
    return lambda w: {"yl": w["yl"] ^ w["c"] ^ j, "c": w["yl"]}


def norm(v, gain):
    return v * lax.rsqrt(jnp.mean(v * v, axis=-1, keepdims=True) + 1e-06) * gain


def silu(v):
    return v / (1.0 + jnp.exp(-v))


def inner_rows(frames, w_ref, acc, part_ref):
    for t in range(3):
        xs = frames[t : t + 4]
        lhs = jnp.concatenate([xs[:, 0], xs[:, 1]], axis=-1).reshape(4 * WIDE, 2 * C)
        rhs = jnp.concatenate(
            [w_ref[t, 1 - i : 3 - i, c].reshape(2 * C, C) for i in range(ROWS) for c in range(3)],
            axis=-1,
        )
        y = jnp.dot(lhs, rhs, preferred_element_type=F32)
        if t == 0:
            acc[...] = y
        else:
            acc[...] += y
    for i in range(ROWS):
        part_ref[i] = summed(acc[:, i * 3 * C : (i + 1) * 3 * C])


def outer_rows(edges, w_ref, part_ref):
    out = []
    for i in range(ROWS):
        lhs = jnp.concatenate([edges[i, t : t + 4] for t in range(3)], axis=-1)
        rhs = jnp.concatenate(
            [w_ref[:, 2 * i, c].reshape(3 * C, C) for c in range(3)], axis=-1
        )
        y = jnp.dot(lhs.reshape(4 * WIDE, 3 * C), rhs, preferred_element_type=F32)
        out.append(part_ref[i] + summed(y))
    return out


def summed(y):
    n = y.shape[0]
    return (
        pltpu.roll(y[:, :C], 1, 0) + y[:, C : 2 * C] + pltpu.roll(y[:, 2 * C :], n - 1, 0)
    )


def windows(v):
    edge = jnp.zeros((v.shape[0], 2, C), F32)
    v = jnp.concatenate([edge, v.astype(F32), edge], axis=1)
    return [v[:, q * COLS : q * COLS + WIDE].astype(BF) for q in range(4)]


def pieces_kernel(at_ref, v_ref, own_ref, near_ref, far_ref, held):
    q = at_ref[0]
    for i, window in enumerate(windows(v_ref[0])):
        held[i] = window
    own_ref[...] = held[q]
    near_ref[...] = held[q ^ 1]
    far_ref[0] = held[q ^ 2]
    far_ref[1] = held[q ^ 3]


def caches_kernel(at_ref, first_ref, second_ref, out_ref, held):
    for n, ref in enumerate((first_ref, second_ref)):
        for f in range(2):
            for i, window in enumerate(windows(ref[f])):
                held[i] = window
            out_ref[2 * n + f] = held[at_ref[0]]


def relay_kernel(near_ref, yo_ref, out_ref):
    out_ref[0] = near_ref[...]
    out_ref[1] = yo_ref[1]


def edges_kernel(at_ref, own_ref, yo_ref, co_ref, c_ref, a_ref, b_ref):
    odd = at_ref[1]
    refs = (own_ref, co_ref.at[0], yo_ref.at[0], co_ref.at[1], c_ref.at[0], c_ref.at[1])
    for k, ref in enumerate(refs):
        top, bottom = ref[0], ref[1]
        a_ref[k] = jnp.where(odd == 0, bottom, top)
        b_ref[k] = jnp.where(odd == 0, top, bottom)


def first_inner_kernel(at_ref, p_ref, yo_ref, co_ref, c_ref, g_ref, w_ref, part_ref, frames, acc):
    q = at_ref[0]
    frames[0:2] = c_ref[0:2]
    gain = g_ref[...]
    for k, own in enumerate((p_ref[...], co_ref[0], yo_ref[0], co_ref[1])):
        frames[2 + (q ^ k)] = silu(norm(own.astype(F32), gain)).astype(BF)
    inner_rows(frames, w_ref, acc, part_ref)


def first_outer_kernel(
    at_ref, part_ref, a_ref, b_ref, c_ref, g1_ref, g2_ref, w_ref,
    out_ref, out_a, out_b, edges,
):
    q, odd = at_ref[0], at_ref[1]
    for at_row, rows in ((1 - odd, a_ref), (odd, b_ref)):
        edges[at_row, 0:2] = rows[4:6]
        for k in range(4):
            v = rows[k].astype(F32)
            edges[at_row, 2 + (q ^ k)] = silu(norm(v, g1_ref[...])).astype(BF)
    place = lax.broadcasted_iota(jnp.int32, (WIDE, 1), 0)
    column = place + COLS * q - 2
    valid = (column >= 0) & (column < 4 * COLS) & (place > 0) & (place < WIDE - 1)
    rows = []
    for i, y in enumerate(outer_rows(edges, w_ref, part_ref)):
        h = silu(norm(y, g2_ref[...])).reshape(4, WIDE, C)
        h = jnp.where(valid[None], h, 0.0)
        out_ref[:, i] = h.astype(BF)
        rows.append(h)
    out_a[0:4] = jnp.where(odd == 0, rows[1], rows[0]).astype(BF)
    out_b[0:4] = jnp.where(odd == 0, rows[0], rows[1]).astype(BF)
    for f in range(2):
        out_a[4 + f] = jnp.where(odd == 0, c_ref[2 + f, 1], c_ref[2 + f, 0])
        out_b[4 + f] = jnp.where(odd == 0, c_ref[2 + f, 0], c_ref[2 + f, 1])


def second_inner_kernel(h_ref, c_ref, w_ref, part_ref, frames, acc):
    frames[0:2] = c_ref[2:4]
    frames[2:6] = h_ref[...]
    inner_rows(frames, w_ref, acc, part_ref)


def second_outer_kernel(
    at_ref, part_ref, a_ref, b_ref, p_ref, yo_ref, co_ref, g_ref, w_ref,
    n0, n1, n2, n3, r0, r1, r23, edges, sums, kept,
):
    q, odd, y = at_ref[0], at_ref[1], at_ref[2]
    for at_row, rows in ((1 - odd, a_ref), (odd, b_ref)):
        edges[at_row, 0:2] = rows[4:6]
        edges[at_row, 2:6] = rows[0:4]
    for i, v in enumerate(outer_rows(edges, w_ref, part_ref)):
        sums[:, i] = v.reshape(4, WIDE, C)
    span = ROWS * WIDE
    for k, latent in enumerate((p_ref[...], co_ref[0], yo_ref[0], co_ref[1])):
        f = q ^ k
        total = (sums[f] + latent.astype(F32)).reshape(span, C)
        total = pltpu.roll(total, span - 2, 0)
        kept[f] = jnp.concatenate([total[0:COLS], total[WIDE : WIDE + COLS]], axis=0)
    for k, n_ref in enumerate((n0, n1, n2, n3)):
        n_ref[...] = norm(kept[y ^ k], g_ref[...]).astype(BF)
    r0[...] = kept[q]
    r1[...] = kept[q ^ 1]
    r23[:SLICE] = kept[q ^ 2]
    r23[SLICE:] = kept[q ^ 3]


SCALAR = pl.BlockSpec(memory_space=pltpu.SMEM)
NEAR = pl.BlockSpec(memory_space=pltpu.VMEM)
PARAMS = pltpu.CompilerParams(vmem_limit_bytes=24 * 1024 * 1024)


def cost(flops, moved):
    return pl.CostEstimate(flops=flops, bytes_accessed=moved, transcendentals=0)


FRAMES = pltpu.VMEM((6, ROWS, WIDE, C), BF)
EDGES = pltpu.VMEM((2, 6, WIDE, C), BF)
ACC = pltpu.VMEM((4 * WIDE, ROWS * 3 * C), F32)
PART = jax.ShapeDtypeStruct((ROWS, 4 * WIDE, C), F32)
EDGE = jax.ShapeDtypeStruct((6, WIDE, C), BF)
HIDDEN = jax.ShapeDtypeStruct((4, ROWS, WIDE, C), BF)
UNIT = 2 * 4 * WIDE * 3 * C * 3 * C


def conv_call(kernel, args, scalars, out_shape, scratch, share, name):
    return pl.pallas_call(
        kernel,
        out_shape=out_shape,
        in_specs=[SCALAR] * scalars + [NEAR] * (len(args) - scalars),
        out_specs=jax.tree.map(lambda _: NEAR, out_shape),
        scratch_shapes=scratch,
        compiler_params=PARAMS,
        cost_estimate=cost(share * UNIT, 6_000_000),
        name=name,
    )(*args)


def project(raw, wq_ref, wkv_ref):
    queries = jnp.dot(raw, wq_ref[...], preferred_element_type=F32).astype(BF)
    queries = lax.dot_general(
        queries, wkv_ref[:, :C], (((1,), (1,)), ((), ())), preferred_element_type=F32
    )
    return (queries * SCALE).astype(BF)


def score(queries, keys):
    return lax.dot_general(queries, keys, (((1,), (1,)), ((), ())), preferred_element_type=F32)


def sweep(queries, keys, acc, state):
    rows = queries.shape[0]
    if state is None:
        peak = jnp.full((rows, 1), -1e30, F32)
        total = jnp.zeros((rows, 1), F32)
        acc[...] = jnp.zeros((rows, C), F32)
    else:
        peak, total = state
    scores = score(queries, keys[0][...])
    for i, block in enumerate(keys):
        following = score(queries, keys[i + 1][...]) if i + 1 < len(keys) else None
        risen = jnp.maximum(peak, jnp.max(scores, axis=1, keepdims=True))
        share = jnp.exp2(peak - risen)
        e = jnp.exp2(scores - risen)
        total = total * share + jnp.sum(e, axis=1, keepdims=True)
        acc[...] = acc[...] * share + jnp.dot(
            e.astype(BF), block[...], preferred_element_type=F32
        )
        peak, scores = risen, following
    return peak, total


def noted(peak, total):
    rows = peak.shape[0]
    return jnp.concatenate(
        [jnp.broadcast_to(peak, (rows, 128)), jnp.broadcast_to(total, (rows, 128))], axis=1
    )


def recalled(stats):
    return (
        jnp.max(stats[:, :128], axis=1, keepdims=True),
        jnp.max(stats[:, 128:], axis=1, keepdims=True),
    )


def packed(peak, total, weighted):
    lane = lax.broadcasted_iota(jnp.int32, (peak.shape[0], 128), 1)
    level = peak + jnp.log2(total)
    first = level.astype(BF).astype(F32)
    second = (level - first).astype(BF).astype(F32)
    third = level - first - second
    side = jnp.where(
        lane == 0, first, jnp.where(lane == 1, second, jnp.where(lane == 2, third, 0.0))
    )
    return jnp.concatenate([(weighted / total).astype(BF), side.astype(BF)], axis=1)


def attend_near_kernel(qa, qb, k0, k1, k2, k3, wq, wkv, out, stats):
    queries = project(jnp.concatenate([qa[...], qb[...]], axis=0), wq, wkv)
    stats[...] = noted(*sweep(queries, (k0, k1, k2, k3), out, None))


def attend_far_kernel(
    qa, qb, weighted, stats, q, own_weighted, own_stats, k0, k1, k2, k3, wq, wkv,
    out_a, out_b, out, acc, own_acc,
):
    acc[...] = weighted[...]
    queries = project(jnp.concatenate([qa[...], qb[...]], axis=0), wq, wkv)
    peak, total = sweep(queries, (k0, k1, k2, k3), acc, recalled(stats))
    result = packed(peak, total, acc[...])
    out_a[...] = result[:BLOCK]
    out_b[...] = result[BLOCK:]
    own_acc[...] = own_weighted[...]
    peak, total = sweep(project(q[...], wq, wkv), (k2, k3), own_acc, recalled(own_stats))
    out[...] = packed(peak, total, own_acc[...])


def attend_all_kernel(q, k0, k1, k2, k3, k4, k5, k6, k7, wq, wkv, out, acc):
    queries = project(q[...], wq, wkv)
    peak, total = sweep(queries, (k0, k1, k2, k3, k4, k5, k6, k7), acc, None)
    out[...] = packed(peak, total, acc[...])


def attend_own_kernel(q, k0, k1, k2, k3, k4, k5, wq, wkv, out, stats):
    queries = project(q[...], wq, wkv)
    stats[...] = noted(*sweep(queries, (k0, k1, k2, k3, k4, k5), out, None))


def attend(kernel, first, keys, weights, out_shape, scratch, flops, name):
    args = list(first) + list(keys) + list(weights)
    return pl.pallas_call(
        kernel,
        out_shape=out_shape,
        in_specs=[NEAR] * len(args),
        out_specs=[NEAR] * len(out_shape),
        scratch_shapes=scratch,
        compiler_params=PARAMS,
        cost_estimate=cost(flops // 8, 2 * BLOCK * C),
        name=name,
    )(*args)


def levels_of(parts):
    return [jnp.sum(p[:, C:].astype(F32), axis=1, keepdims=True) for p in parts]


def merge_first_kernel(p0, p1, out, stats):
    levels = levels_of((p0, p1))
    peak = jnp.maximum(*levels)
    shares = [jnp.exp2(level - peak) for level in levels]
    out[...] = p0[:, :C].astype(F32) * shares[0] + p1[:, :C].astype(F32) * shares[1]
    stats[...] = noted(peak, shares[0] + shares[1])


def merge_first_call(own, across):
    return pl.pallas_call(
        merge_first_kernel,
        in_specs=[NEAR] * 2,
        out_specs=[NEAR] * 2,
        out_shape=[
            jax.ShapeDtypeStruct((BLOCK, C), F32),
            jax.ShapeDtypeStruct((BLOCK, 256), F32),
        ],
        compiler_params=PARAMS,
        name="merge_first",
    )(own, across)


def merge_kernel(at_ref, weighted, stats, p2, p3, wkv_ref, out_a, out_b):
    parts = (p2, p3)
    begun, total = recalled(stats)
    levels = levels_of(parts)
    peak = jnp.maximum(begun, jnp.maximum(*levels))
    share = jnp.exp2(begun - peak)
    mixed, total = weighted[...] * share, total * share
    for part, level in zip(parts, levels):
        share = jnp.exp2(level - peak)
        mixed += part[:, :C].astype(F32) * share
        total += share
    mixed = mixed / total
    y = jnp.dot(mixed.astype(BF), wkv_ref[:, C:], preferred_element_type=F32)
    even = jnp.concatenate([y[:SLICE], y[2 * SLICE : 3 * SLICE]], axis=0)
    odd = jnp.concatenate([y[SLICE : 2 * SLICE], y[3 * SLICE :]], axis=0)
    core = at_ref[3]
    out_a[...] = jnp.where(core == 0, even, odd).astype(BF)
    out_b[...] = jnp.where(core == 0, odd, even).astype(BF)


def merge_call(at, parts, wkv):
    return pl.pallas_call(
        merge_kernel,
        in_specs=[SCALAR] + [NEAR] * 5,
        out_specs=[NEAR] * 2,
        out_shape=[jax.ShapeDtypeStruct((HALF, C), BF)] * 2,
        compiler_params=PARAMS,
        name="merge",
    )(at, *parts, wkv)


def final_kernel(at_ref, a_ref, b_ref, r0, ry, rc, wo_ref, out_ref, parts):
    frame, low = at_ref[0], at_ref[4]
    ya = jnp.dot(a_ref[...], wo_ref[...], preferred_element_type=F32)
    yb = jnp.dot(b_ref[...], wo_ref[...], preferred_element_type=F32)
    even, odd = jnp.where(low == 0, ya, yb), jnp.where(low == 0, yb, ya)
    parts[0] = even[:SLICE] + r0[...]
    parts[1] = odd[:SLICE] + rc[:SLICE]
    parts[2] = even[SLICE:] + ry[:SLICE]
    parts[3] = odd[SLICE:] + rc[SLICE:]
    for q in range(4):
        part = parts[frame ^ q]
        out_ref[0, 0, q * COLS : (q + 1) * COLS] = part[:COLS]
        out_ref[0, 1, q * COLS : (q + 1) * COLS] = part[COLS:]


def final_call(at, a, b, r0, ry, rc, wo):
    return pl.pallas_call(
        final_kernel,
        in_specs=[SCALAR] + [NEAR] * 6,
        out_specs=NEAR,
        out_shape=jax.ShapeDtypeStruct((1, ROWS, 4 * COLS, C), F32),
        scratch_shapes=[pltpu.VMEM((4, SLICE, C), F32)],
        compiler_params=PARAMS,
        name="final",
    )(at, a, b, r0, ry, rc, wo)


def shards(
    latent, cache_first, cache_second, gain_first, conv_first, gain_second, conv_second,
    gain_attention, query_weight, keyvalue_weight, out_weight,
):
    low, high, core = (lax.axis_index(a) for a in ("yl", "yh", "c"))
    member = high * 2 + core
    odd = lax.axis_index("z") % 2
    at = jnp.stack([member, odd, high * 2 + low, core, low]).astype(jnp.int32)

    both = jax.ShapeDtypeStruct((ROWS, WIDE, C), BF)
    two = jax.ShapeDtypeStruct((2, ROWS, WIDE, C), BF)
    held = [pltpu.VMEM((4, ROWS, WIDE, C), BF)]
    pieces, near, far = conv_call(
        pieces_kernel, (at, latent), 1, [both, both, two], held, 0, "pieces"
    )
    yo = send(far, ("yh",), other("yh"))
    caches = conv_call(
        caches_kernel, (at, cache_first, cache_second), 1, HIDDEN, held, 0, "caches"
    )
    near, caches = lax.optimization_barrier((near, caches))
    co = conv_call(relay_kernel, (near, yo), 0, two, [], 0, "relay")
    co = send(co, ("c",), other("c"))

    a, b = conv_call(edges_kernel, (at, pieces, yo, co, caches), 1, [EDGE, EDGE], [], 0, "edges")
    a = send(a, AXES, row_swap(False))
    b = send(b, AXES, row_swap(True))
    gain1, gain2, gain3 = gain_first, gain_second, gain_attention
    part = conv_call(
        first_inner_kernel, (at, pieces, yo, co, caches, gain1, conv_first), 1, PART,
        [FRAMES, ACC], 6, "first_inner",
    )
    hidden, ha, hb = conv_call(
        first_outer_kernel, (at, part, a, b, caches, gain1, gain2, conv_first), 1,
        [HIDDEN, EDGE, EDGE], [EDGES], 2, "first_outer",
    )
    ha = send(ha, AXES, row_swap(False))
    hb = send(hb, AXES, row_swap(True))
    part = conv_call(
        second_inner_kernel, (hidden, caches, conv_second), 0, PART, [FRAMES, ACC], 6,
        "second_inner",
    )
    slice_of = lambda n, kind: jax.ShapeDtypeStruct((n * SLICE, C), kind)
    n0, n1, n2, n3, r0, r1, r23 = conv_call(
        second_outer_kernel,
        (at, part, ha, hb, pieces, yo, co, gain3, conv_second), 1,
        [slice_of(1, BF)] * 4 + [slice_of(1, F32)] * 2 + [slice_of(2, F32)],
        [EDGES, pltpu.VMEM((4, ROWS, WIDE, C), F32), pltpu.VMEM((4, SLICE, C), F32)], 2,
        "second_outer",
    )

    group = ("yl", "yh")
    block = jnp.concatenate([n0] + [send(n, group, to_plane(k + 1)) for k, n in enumerate((n1, n2, n3))])
    lines = ("x", "z", "c")
    cross = lambda v: send(v, ("c",), other("c"))
    keyed = lambda v, turn: send(v, lines, line_swap(turn, True))
    asked = lambda v, turn: send(v, lines, line_swap(turn, False))
    p0 = block
    a0, b0 = keyed(p0, False), keyed(p0, True)
    qa, qb = asked(p0, False), asked(p0, True)
    p1 = cross(p0)
    ab, qo = keyed(a0, True), asked(qa, True)
    a1, b1 = cross(qa), cross(qb)
    weights = (query_weight, keyvalue_weight)

    near_keys = [p0, p1, a0, b0]
    unit = 4 * BLOCK * BLOCK * C
    wide = jax.ShapeDtypeStruct((BLOCK, C + 128), BF)
    begun = lambda n: [
        jax.ShapeDtypeStruct((n * BLOCK, C), F32),
        jax.ShapeDtypeStruct((n * BLOCK, 256), F32),
    ]
    weighted, stats = attend(
        attend_near_kernel, [qa, qb], near_keys, weights, begun(2), [], 8 * unit, "attend_near"
    )
    after = lambda v, mark: lax.optimization_barrier((v, mark))[0]
    ba = cross(after(qo, stats))
    ry = send(after(r23, stats), ("yh",), other("yh"))
    own_weighted, own_stats = attend(
        attend_own_kernel, [after(p0, stats)], near_keys + [a1, b1], weights, begun(1), [],
        6 * unit, "attend_own",
    )
    (to,) = attend(
        attend_all_kernel, [after(qo, own_stats)], near_keys + [a1, b1, ab, ba], weights, [wide],
        [pltpu.VMEM((BLOCK, C), F32)], 8 * unit, "attend_across",
    )
    sa, sb, own = attend(
        attend_far_kernel,
        [after(qa, (to, ry)), qb, weighted, stats, p0, own_weighted, own_stats],
        [a1, b1, ab, ba], weights, [wide] * 3,
        [pltpu.VMEM((2 * BLOCK, C), F32), pltpu.VMEM((BLOCK, C), F32)], 10 * unit, "attend_far",
    )
    to = send(to, lines, line_across)
    rc_from = after(ry, sa)
    sa, sb = asked(sa, False), asked(sb, True)
    rc = cross(jnp.concatenate([r1, rc_from[SLICE:]]))
    to_a, to_b = merge_call(at, (*merge_first_call(own, to), sa, sb), keyvalue_weight)
    home = ("yl", "c")
    to_a, to_b = send(to_a, home, to_home(0)), send(to_b, home, to_home(1))
    return final_call(at, to_a, to_b, r0, ry, rc, out_weight)


def solution(mesh):
    fine = Mesh(mesh.devices.reshape([SIZES[a] for a in AXES]), AXES)
    frames, rows = ("yh", "c"), ("x", "yl", "z")
    in_specs = (P(frames, rows), P(None, rows), P(None, rows)) + (P(),) * 8
    return jax.shard_map(
        shards, mesh=fine, in_specs=in_specs, out_specs=P(frames, rows), check_vma=False
    )
```

```python
import functools
import math

import jax
import jax.numpy as jnp
from jax import lax
from jax.experimental import pallas as pl
from jax.experimental.pallas import tpu as pltpu
from jax.sharding import Mesh
from jax.sharding import PartitionSpec as P

C = 384
COLS = 60
WIDE = 64
ROWS = 2
SLICE = ROWS * COLS
BLOCK = 4 * SLICE
HALF = BLOCK // 2
AXES = ("x", "yl", "z", "yh", "c")
SIZES = {"x": 4, "yl": 2, "z": 4, "yh": 2, "c": 2}
BF = jnp.bfloat16
F32 = jnp.float32
SCALE = math.log2(math.e) / math.sqrt(C)


def routes(axes, target):
    sizes = [SIZES[a] for a in axes]
    total = math.prod(sizes)
    pairs = []
    for source in range(total):
        rest, where = source, {}
        for a, n in zip(reversed(axes), reversed(sizes)):
            where[a] = rest % n
            rest //= n
        there = target(dict(where))
        if there is None:
            continue
        index = 0
        for a, n in zip(axes, sizes):
            index = index * n + there[a] % n
        pairs.append((source, index))
    return pairs


def send(value, axes, target):
    return lax.ppermute(value, axes, routes(axes, target))


def row_swap(odd):
    def target(w):
        row = (w["x"] * 2 + w["yl"]) * 4 + w["z"]
        row = ((row + 1) ^ 1) - 1 if odd else row ^ 1
        if row < 0 or row > 31:
            return None
        return {"x": row // 8, "yl": row // 4 % 2, "z": row % 4, "yh": w["yh"], "c": w["c"]}

    return target


def other(axis):
    return lambda w: {axis: 1 - w[axis]}


def to_plane(k):
    def target(w):
        frame = (w["yh"] * 2 + w["yl"]) ^ k
        return {"yh": frame // 2, "yl": frame % 2}

    return target


def line_swap(odd, key_line):
    def target(w):
        axis = "x" if (w["c"] == 0) == key_line else "z"
        w[axis] = (w[axis] + 1) % 4 ^ 1
        w[axis] = (w[axis] - 1) % 4
        return w

    def even(w):
        axis = "x" if (w["c"] == 0) == key_line else "z"
        w[axis] ^= 1
        return w

    return target if odd else even


def line_across(w):
    axis = "z" if w["c"] == 0 else "x"
    w[axis] = (w[axis] + 2) % 4
    return w


def to_home(j):
    return lambda w: {"yl": w["yl"] ^ w["c"] ^ j, "c": w["yl"]}


def norm(v, gain):
    return v * lax.rsqrt(jnp.mean(v * v, axis=-1, keepdims=True) + 1e-06) * gain


def silu(v):
    return v / (1.0 + jnp.exp(-v))


def inner_rows(frames, w_ref, acc, part_ref):
    for t in range(3):
        xs = frames[t : t + 4]
        lhs = jnp.concatenate([xs[:, 0], xs[:, 1]], axis=-1).reshape(4 * WIDE, 2 * C)
        rhs = jnp.concatenate(
            [w_ref[t, 1 - i : 3 - i, c].reshape(2 * C, C) for i in range(ROWS) for c in range(3)],
            axis=-1,
        )
        y = jnp.dot(lhs, rhs, preferred_element_type=F32)
        if t == 0:
            acc[...] = y
        else:
            acc[...] += y
    for i in range(ROWS):
        part_ref[i] = summed(acc[:, i * 3 * C : (i + 1) * 3 * C])


def outer_rows(edges, w_ref, part_ref):
    out = []
    for i in range(ROWS):
        lhs = jnp.concatenate([edges[i, t : t + 4] for t in range(3)], axis=-1)
        rhs = jnp.concatenate(
            [w_ref[:, 2 * i, c].reshape(3 * C, C) for c in range(3)], axis=-1
        )
        y = jnp.dot(lhs.reshape(4 * WIDE, 3 * C), rhs, preferred_element_type=F32)
        out.append(part_ref[i] + summed(y))
    return out


def summed(y):
    n = y.shape[0]
    return (
        pltpu.roll(y[:, :C], 1, 0) + y[:, C : 2 * C] + pltpu.roll(y[:, 2 * C :], n - 1, 0)
    )


def windows(v):
    edge = jnp.zeros((v.shape[0], 2, C), F32)
    v = jnp.concatenate([edge, v.astype(F32), edge], axis=1)
    return [v[:, q * COLS : q * COLS + WIDE].astype(BF) for q in range(4)]


def pieces_kernel(at_ref, v_ref, own_ref, near_ref, far_ref, held):
    q = at_ref[0]
    for i, window in enumerate(windows(v_ref[0])):
        held[i] = window
    own_ref[...] = held[q]
    near_ref[...] = held[q ^ 1]
    far_ref[0] = held[q ^ 2]
    far_ref[1] = held[q ^ 3]


def caches_kernel(at_ref, first_ref, second_ref, out_ref, held):
    for n, ref in enumerate((first_ref, second_ref)):
        for f in range(2):
            for i, window in enumerate(windows(ref[f])):
                held[i] = window
            out_ref[2 * n + f] = held[at_ref[0]]


def relay_kernel(near_ref, yo_ref, out_ref):
    out_ref[0] = near_ref[...]
    out_ref[1] = yo_ref[1]


def edges_kernel(at_ref, own_ref, yo_ref, co_ref, c_ref, a_ref, b_ref):
    odd = at_ref[1]
    refs = (own_ref, co_ref.at[0], yo_ref.at[0], co_ref.at[1], c_ref.at[0], c_ref.at[1])
    for k, ref in enumerate(refs):
        top, bottom = ref[0], ref[1]
        a_ref[k] = jnp.where(odd == 0, bottom, top)
        b_ref[k] = jnp.where(odd == 0, top, bottom)


def first_inner_kernel(at_ref, p_ref, yo_ref, co_ref, c_ref, g_ref, w_ref, part_ref, frames, acc):
    q = at_ref[0]
    frames[0:2] = c_ref[0:2]
    gain = g_ref[...]
    for k, own in enumerate((p_ref[...], co_ref[0], yo_ref[0], co_ref[1])):
        frames[2 + (q ^ k)] = silu(norm(own.astype(F32), gain)).astype(BF)
    inner_rows(frames, w_ref, acc, part_ref)


def first_outer_kernel(
    at_ref, part_ref, a_ref, b_ref, c_ref, g1_ref, g2_ref, w_ref,
    out_ref, out_a, out_b, edges,
):
    q, odd = at_ref[0], at_ref[1]
    for at_row, rows in ((1 - odd, a_ref), (odd, b_ref)):
        edges[at_row, 0:2] = rows[4:6]
        for k in range(4):
            v = rows[k].astype(F32)
            edges[at_row, 2 + (q ^ k)] = silu(norm(v, g1_ref[...])).astype(BF)
    place = lax.broadcasted_iota(jnp.int32, (WIDE, 1), 0)
    column = place + COLS * q - 2
    valid = (column >= 0) & (column < 4 * COLS) & (place > 0) & (place < WIDE - 1)
    rows = []
    for i, y in enumerate(outer_rows(edges, w_ref, part_ref)):
        h = silu(norm(y, g2_ref[...])).reshape(4, WIDE, C)
        h = jnp.where(valid[None], h, 0.0)
        out_ref[:, i] = h.astype(BF)
        rows.append(h)
    out_a[0:4] = jnp.where(odd == 0, rows[1], rows[0]).astype(BF)
    out_b[0:4] = jnp.where(odd == 0, rows[0], rows[1]).astype(BF)
    for f in range(2):
        out_a[4 + f] = jnp.where(odd == 0, c_ref[2 + f, 1], c_ref[2 + f, 0])
        out_b[4 + f] = jnp.where(odd == 0, c_ref[2 + f, 0], c_ref[2 + f, 1])


def second_inner_kernel(h_ref, c_ref, w_ref, part_ref, frames, acc):
    frames[0:2] = c_ref[2:4]
    frames[2:6] = h_ref[...]
    inner_rows(frames, w_ref, acc, part_ref)


def second_outer_kernel(
    at_ref, part_ref, a_ref, b_ref, p_ref, yo_ref, co_ref, g_ref, w_ref,
    n0, n1, n2, n3, r0, r1, r23, edges, sums, kept,
):
    q, odd, y = at_ref[0], at_ref[1], at_ref[2]
    for at_row, rows in ((1 - odd, a_ref), (odd, b_ref)):
        edges[at_row, 0:2] = rows[4:6]
        edges[at_row, 2:6] = rows[0:4]
    for i, v in enumerate(outer_rows(edges, w_ref, part_ref)):
        sums[:, i] = v.reshape(4, WIDE, C)
    span = ROWS * WIDE
    for k, latent in enumerate((p_ref[...], co_ref[0], yo_ref[0], co_ref[1])):
        f = q ^ k
        total = (sums[f] + latent.astype(F32)).reshape(span, C)
        total = pltpu.roll(total, span - 2, 0)
        kept[f] = jnp.concatenate([total[0:COLS], total[WIDE : WIDE + COLS]], axis=0)
    for k, n_ref in enumerate((n0, n1, n2, n3)):
        n_ref[...] = norm(kept[y ^ k], g_ref[...]).astype(BF)
    r0[...] = kept[q]
    r1[...] = kept[q ^ 1]
    r23[:SLICE] = kept[q ^ 2]
    r23[SLICE:] = kept[q ^ 3]


SCALAR = pl.BlockSpec(memory_space=pltpu.SMEM)
NEAR = pl.BlockSpec(memory_space=pltpu.VMEM)
PARAMS = pltpu.CompilerParams(vmem_limit_bytes=24 * 1024 * 1024)


def cost(flops, moved):
    return pl.CostEstimate(flops=flops, bytes_accessed=moved, transcendentals=0)


FRAMES = pltpu.VMEM((6, ROWS, WIDE, C), BF)
EDGES = pltpu.VMEM((2, 6, WIDE, C), BF)
ACC = pltpu.VMEM((4 * WIDE, ROWS * 3 * C), F32)
PART = jax.ShapeDtypeStruct((ROWS, 4 * WIDE, C), F32)
EDGE = jax.ShapeDtypeStruct((6, WIDE, C), BF)
HIDDEN = jax.ShapeDtypeStruct((4, ROWS, WIDE, C), BF)
UNIT = 2 * 4 * WIDE * 3 * C * 3 * C


def conv_call(kernel, args, scalars, out_shape, scratch, share, name):
    return pl.pallas_call(
        kernel,
        out_shape=out_shape,
        in_specs=[SCALAR] * scalars + [NEAR] * (len(args) - scalars),
        out_specs=jax.tree.map(lambda _: NEAR, out_shape),
        scratch_shapes=scratch,
        compiler_params=PARAMS,
        cost_estimate=cost(share * UNIT, 6_000_000),
        name=name,
    )(*args)


def project(raw, wq_ref, wkv_ref):
    queries = jnp.dot(raw, wq_ref[...], preferred_element_type=F32).astype(BF)
    queries = lax.dot_general(
        queries, wkv_ref[:, :C], (((1,), (1,)), ((), ())), preferred_element_type=F32
    )
    return (queries * SCALE).astype(BF)


def score(queries, keys):
    return lax.dot_general(queries, keys, (((1,), (1,)), ((), ())), preferred_element_type=F32)


def sweep(queries, keys, acc, state):
    rows = queries.shape[0]
    if state is None:
        peak = jnp.full((rows, 1), -1e30, F32)
        total = jnp.zeros((rows, 1), F32)
        acc[...] = jnp.zeros((rows, C), F32)
    else:
        peak, total = state
    scores = score(queries, keys[0][...])
    for i, block in enumerate(keys):
        following = score(queries, keys[i + 1][...]) if i + 1 < len(keys) else None
        risen = jnp.maximum(peak, jnp.max(scores, axis=1, keepdims=True))
        share = jnp.exp2(peak - risen)
        e = jnp.exp2(scores - risen)
        total = total * share + jnp.sum(e, axis=1, keepdims=True)
        acc[...] = acc[...] * share + jnp.dot(
            e.astype(BF), block[...], preferred_element_type=F32
        )
        peak, scores = risen, following
    return peak, total


def noted(peak, total):
    rows = peak.shape[0]
    return jnp.concatenate(
        [jnp.broadcast_to(peak, (rows, 128)), jnp.broadcast_to(total, (rows, 128))], axis=1
    )


def recalled(stats):
    return (
        jnp.max(stats[:, :128], axis=1, keepdims=True),
        jnp.max(stats[:, 128:], axis=1, keepdims=True),
    )


def packed(peak, total, weighted):
    lane = lax.broadcasted_iota(jnp.int32, (peak.shape[0], 128), 1)
    level = peak + jnp.log2(total)
    first = level.astype(BF).astype(F32)
    second = (level - first).astype(BF).astype(F32)
    third = level - first - second
    side = jnp.where(
        lane == 0, first, jnp.where(lane == 1, second, jnp.where(lane == 2, third, 0.0))
    )
    return jnp.concatenate([(weighted / total).astype(BF), side.astype(BF)], axis=1)


def attend_near_kernel(qa, qb, k0, k1, k2, k3, wq, wkv, out, stats):
    queries = project(jnp.concatenate([qa[...], qb[...]], axis=0), wq, wkv)
    stats[...] = noted(*sweep(queries, (k0, k1, k2, k3), out, None))


def attend_far_kernel(qa, qb, weighted, stats, k0, k1, k2, k3, wq, wkv, out_a, out_b, acc):
    acc[...] = weighted[...]
    queries = project(jnp.concatenate([qa[...], qb[...]], axis=0), wq, wkv)
    peak, total = sweep(queries, (k0, k1, k2, k3), acc, recalled(stats))
    result = packed(peak, total, acc[...])
    out_a[...] = result[:BLOCK]
    out_b[...] = result[BLOCK:]


def attend_all_kernel(q, k0, k1, k2, k3, k4, k5, k6, k7, wq, wkv, out, acc):
    queries = project(q[...], wq, wkv)
    peak, total = sweep(queries, (k0, k1, k2, k3, k4, k5, k6, k7), acc, None)
    out[...] = packed(peak, total, acc[...])


def attend_own_kernel(q, k0, k1, wq, wkv, out, stats):
    queries = project(q[...], wq, wkv)
    stats[...] = noted(*sweep(queries, (k0, k1), out, None))


def attend_more_kernel(q, weighted, before, k0, k1, k2, k3, wq, wkv, out, stats):
    out[...] = weighted[...]
    queries = project(q[...], wq, wkv)
    stats[...] = noted(*sweep(queries, (k0, k1, k2, k3), out, recalled(before)))


def attend_rest_kernel(q, weighted, stats, k6, k7, wq, wkv, out, acc):
    acc[...] = weighted[...]
    peak, total = sweep(project(q[...], wq, wkv), (k6, k7), acc, recalled(stats))
    out[...] = packed(peak, total, acc[...])


def attend(kernel, first, keys, weights, out_shape, scratch, flops, name):
    args = list(first) + list(keys) + list(weights)
    return pl.pallas_call(
        kernel,
        out_shape=out_shape,
        in_specs=[NEAR] * len(args),
        out_specs=[NEAR] * len(out_shape),
        scratch_shapes=scratch,
        compiler_params=PARAMS,
        cost_estimate=cost(flops // 8, 2 * BLOCK * C),
        name=name,
    )(*args)


def levels_of(parts):
    return [jnp.sum(p[:, C:].astype(F32), axis=1, keepdims=True) for p in parts]


def merge_first_kernel(p0, p1, out, stats):
    levels = levels_of((p0, p1))
    peak = jnp.maximum(*levels)
    shares = [jnp.exp2(level - peak) for level in levels]
    out[...] = p0[:, :C].astype(F32) * shares[0] + p1[:, :C].astype(F32) * shares[1]
    stats[...] = noted(peak, shares[0] + shares[1])


def merge_first_call(own, across):
    return pl.pallas_call(
        merge_first_kernel,
        in_specs=[NEAR] * 2,
        out_specs=[NEAR] * 2,
        out_shape=[
            jax.ShapeDtypeStruct((BLOCK, C), F32),
            jax.ShapeDtypeStruct((BLOCK, 256), F32),
        ],
        compiler_params=PARAMS,
        name="merge_first",
    )(own, across)


def merge_kernel(at_ref, weighted, stats, p2, p3, wkv_ref, out_a, out_b):
    parts = (p2, p3)
    begun, total = recalled(stats)
    levels = levels_of(parts)
    peak = jnp.maximum(begun, jnp.maximum(*levels))
    share = jnp.exp2(begun - peak)
    mixed, total = weighted[...] * share, total * share
    for part, level in zip(parts, levels):
        share = jnp.exp2(level - peak)
        mixed += part[:, :C].astype(F32) * share
        total += share
    mixed = mixed / total
    y = jnp.dot(mixed.astype(BF), wkv_ref[:, C:], preferred_element_type=F32)
    even = jnp.concatenate([y[:SLICE], y[2 * SLICE : 3 * SLICE]], axis=0)
    odd = jnp.concatenate([y[SLICE : 2 * SLICE], y[3 * SLICE :]], axis=0)
    core = at_ref[3]
    out_a[...] = jnp.where(core == 0, even, odd).astype(BF)
    out_b[...] = jnp.where(core == 0, odd, even).astype(BF)


def merge_call(at, parts, wkv):
    return pl.pallas_call(
        merge_kernel,
        in_specs=[SCALAR] + [NEAR] * 5,
        out_specs=[NEAR] * 2,
        out_shape=[jax.ShapeDtypeStruct((HALF, C), BF)] * 2,
        compiler_params=PARAMS,
        name="merge",
    )(at, *parts, wkv)


def final_kernel(at_ref, a_ref, b_ref, r0, ry, rc, wo_ref, out_ref, parts):
    frame, low = at_ref[0], at_ref[4]
    ya = jnp.dot(a_ref[...], wo_ref[...], preferred_element_type=F32)
    yb = jnp.dot(b_ref[...], wo_ref[...], preferred_element_type=F32)
    even, odd = jnp.where(low == 0, ya, yb), jnp.where(low == 0, yb, ya)
    parts[0] = even[:SLICE] + r0[...]
    parts[1] = odd[:SLICE] + rc[:SLICE]
    parts[2] = even[SLICE:] + ry[:SLICE]
    parts[3] = odd[SLICE:] + rc[SLICE:]
    for q in range(4):
        part = parts[frame ^ q]
        out_ref[0, 0, q * COLS : (q + 1) * COLS] = part[:COLS]
        out_ref[0, 1, q * COLS : (q + 1) * COLS] = part[COLS:]


def final_call(at, a, b, r0, ry, rc, wo):
    return pl.pallas_call(
        final_kernel,
        in_specs=[SCALAR] + [NEAR] * 6,
        out_specs=NEAR,
        out_shape=jax.ShapeDtypeStruct((1, ROWS, 4 * COLS, C), F32),
        scratch_shapes=[pltpu.VMEM((4, SLICE, C), F32)],
        compiler_params=PARAMS,
        name="final",
    )(at, a, b, r0, ry, rc, wo)


def shards(
    latent, cache_first, cache_second, gain_first, conv_first, gain_second, conv_second,
    gain_attention, query_weight, keyvalue_weight, out_weight,
):
    low, high, core = (lax.axis_index(a) for a in ("yl", "yh", "c"))
    member = high * 2 + core
    odd = lax.axis_index("z") % 2
    at = jnp.stack([member, odd, high * 2 + low, core, low]).astype(jnp.int32)

    both = jax.ShapeDtypeStruct((ROWS, WIDE, C), BF)
    two = jax.ShapeDtypeStruct((2, ROWS, WIDE, C), BF)
    held = [pltpu.VMEM((4, ROWS, WIDE, C), BF)]
    pieces, near, far = conv_call(
        pieces_kernel, (at, latent), 1, [both, both, two], held, 0, "pieces"
    )
    yo = send(far, ("yh",), other("yh"))
    caches = conv_call(
        caches_kernel, (at, cache_first, cache_second), 1, HIDDEN, held, 0, "caches"
    )
    near, caches = lax.optimization_barrier((near, caches))
    co = conv_call(relay_kernel, (near, yo), 0, two, [], 0, "relay")
    co = send(co, ("c",), other("c"))

    a, b = conv_call(edges_kernel, (at, pieces, yo, co, caches), 1, [EDGE, EDGE], [], 0, "edges")
    a = send(a, AXES, row_swap(False))
    b = send(b, AXES, row_swap(True))
    gain1, gain2, gain3 = gain_first, gain_second, gain_attention
    part = conv_call(
        first_inner_kernel, (at, pieces, yo, co, caches, gain1, conv_first), 1, PART,
        [FRAMES, ACC], 6, "first_inner",
    )
    hidden, ha, hb = conv_call(
        first_outer_kernel, (at, part, a, b, caches, gain1, gain2, conv_first), 1,
        [HIDDEN, EDGE, EDGE], [EDGES], 2, "first_outer",
    )
    ha = send(ha, AXES, row_swap(False))
    hb = send(hb, AXES, row_swap(True))
    part = conv_call(
        second_inner_kernel, (hidden, caches, conv_second), 0, PART, [FRAMES, ACC], 6,
        "second_inner",
    )
    slice_of = lambda n, kind: jax.ShapeDtypeStruct((n * SLICE, C), kind)
    n0, n1, n2, n3, r0, r1, r23 = conv_call(
        second_outer_kernel,
        (at, part, ha, hb, pieces, yo, co, gain3, conv_second), 1,
        [slice_of(1, BF)] * 4 + [slice_of(1, F32)] * 2 + [slice_of(2, F32)],
        [EDGES, pltpu.VMEM((4, ROWS, WIDE, C), F32), pltpu.VMEM((4, SLICE, C), F32)], 2,
        "second_outer",
    )

    group = ("yl", "yh")
    block = jnp.concatenate([n0] + [send(n, group, to_plane(k + 1)) for k, n in enumerate((n1, n2, n3))])
    lines = ("x", "z", "c")
    cross = lambda v: send(v, ("c",), other("c"))
    keyed = lambda v, turn: send(v, lines, line_swap(turn, True))
    asked = lambda v, turn: send(v, lines, line_swap(turn, False))
    p0 = block
    a0, b0 = keyed(p0, False), keyed(p0, True)
    qa, qb = asked(p0, False), asked(p0, True)
    p1 = cross(p0)
    ab, qo = keyed(a0, True), asked(qb, False)
    a1, b1 = cross(qa), cross(qb)
    weights = (query_weight, keyvalue_weight)

    near_keys = [p0, p1, a0, b0]
    unit = 4 * BLOCK * BLOCK * C
    wide = jax.ShapeDtypeStruct((BLOCK, C + 128), BF)
    begun = lambda n: [
        jax.ShapeDtypeStruct((n * BLOCK, C), F32),
        jax.ShapeDtypeStruct((n * BLOCK, 256), F32),
    ]
    after = lambda v, mark: lax.optimization_barrier((v, mark))[0]
    own_weighted, own_stats = attend(
        attend_own_kernel, [p0], [p0, p1], weights, begun(1), [], 2 * unit, "attend_own"
    )
    weighted, stats = attend(
        attend_near_kernel, [after(qa, own_stats), qb], near_keys, weights, begun(2), [], 8 * unit, "attend_near"
    )
    ba = cross(after(qo, stats))
    ry = send(after(r23, stats), ("yh",), other("yh"))
    own_weighted, own_stats = attend(
        attend_more_kernel, [after(p0, stats), own_weighted, own_stats], [a0, b0, a1, b1],
        weights, begun(1), [], 4 * unit, "attend_more",
    )
    (to,) = attend(
        attend_all_kernel, [after(qo, own_stats)], near_keys + [a1, b1, ab, ba], weights, [wide],
        [pltpu.VMEM((BLOCK, C), F32)], 8 * unit, "attend_across",
    )
    sa, sb = attend(
        attend_far_kernel, [after(qa, (to, ry)), qb, weighted, stats], [a1, b1, ab, ba], weights,
        [wide] * 2, [pltpu.VMEM((2 * BLOCK, C), F32)], 8 * unit, "attend_far",
    )
    (own,) = attend(
        attend_rest_kernel, [after(p0, sa), own_weighted, own_stats], [ab, ba], weights, [wide],
        [pltpu.VMEM((BLOCK, C), F32)], 2 * unit, "attend_rest",
    )
    to = send(to, lines, line_across)
    rc_from = after(ry, sa)
    sa, sb = asked(sa, False), asked(sb, True)
    rc = cross(jnp.concatenate([r1, rc_from[SLICE:]]))
    to_a, to_b = merge_call(at, (*merge_first_call(own, to), sa, sb), keyvalue_weight)
    home = ("yl", "c")
    to_a, to_b = send(to_a, home, to_home(0)), send(to_b, home, to_home(1))
    return final_call(at, to_a, to_b, r0, ry, rc, out_weight)


def solution(mesh):
    fine = Mesh(mesh.devices.reshape([SIZES[a] for a in AXES]), AXES)
    frames, rows = ("yh", "c"), ("x", "yl", "z")
    in_specs = (P(frames, rows), P(None, rows), P(None, rows)) + (P(),) * 8
    return jax.shard_map(
        shards, mesh=fine, in_specs=in_specs, out_specs=P(frames, rows), check_vma=False
    )
```

```python
import functools
import math

import jax
import jax.numpy as jnp
from jax import lax
from jax.experimental import pallas as pl
from jax.experimental.pallas import tpu as pltpu
from jax.sharding import Mesh
from jax.sharding import PartitionSpec as P

C = 384
COLS = 60
WIDE = 64
ROWS = 2
SLICE = ROWS * COLS
BLOCK = 4 * SLICE
HALF = BLOCK // 2
AXES = ("x", "yl", "z", "yh", "c")
SIZES = {"x": 4, "yl": 2, "z": 4, "yh": 2, "c": 2}
BF = jnp.bfloat16
F32 = jnp.float32
SCALE = math.log2(math.e) / math.sqrt(C)


def routes(axes, target):
    sizes = [SIZES[a] for a in axes]
    total = math.prod(sizes)
    pairs = []
    for source in range(total):
        rest, where = source, {}
        for a, n in zip(reversed(axes), reversed(sizes)):
            where[a] = rest % n
            rest //= n
        there = target(dict(where))
        if there is None:
            continue
        index = 0
        for a, n in zip(axes, sizes):
            index = index * n + there[a] % n
        pairs.append((source, index))
    return pairs


def send(value, axes, target):
    return lax.ppermute(value, axes, routes(axes, target))


def row_swap(odd):
    def target(w):
        row = (w["x"] * 2 + w["yl"]) * 4 + w["z"]
        row = ((row + 1) ^ 1) - 1 if odd else row ^ 1
        if row < 0 or row > 31:
            return None
        return {"x": row // 8, "yl": row // 4 % 2, "z": row % 4, "yh": w["yh"], "c": w["c"]}

    return target


def other(axis):
    return lambda w: {axis: 1 - w[axis]}


def to_plane(k):
    def target(w):
        frame = (w["yh"] * 2 + w["yl"]) ^ k
        return {"yh": frame // 2, "yl": frame % 2}

    return target


def line_swap(odd, key_line):
    def target(w):
        axis = "x" if (w["c"] == 0) == key_line else "z"
        w[axis] = (w[axis] + 1) % 4 ^ 1
        w[axis] = (w[axis] - 1) % 4
        return w

    def even(w):
        axis = "x" if (w["c"] == 0) == key_line else "z"
        w[axis] ^= 1
        return w

    return target if odd else even


def line_across(w):
    axis = "z" if w["c"] == 0 else "x"
    w[axis] = (w[axis] + 2) % 4
    return w


def to_home(j):
    return lambda w: {"yl": w["yl"] ^ w["c"] ^ j, "c": w["yl"]}


def norm(v, gain):
    return v * lax.rsqrt(jnp.mean(v * v, axis=-1, keepdims=True) + 1e-06) * gain


def silu(v):
    return v / (1.0 + jnp.exp(-v))


def inner_rows(frames, w_ref, acc, part_ref):
    for t in range(3):
        xs = frames[t : t + 4]
        lhs = jnp.concatenate([xs[:, 0], xs[:, 1]], axis=-1).reshape(4 * WIDE, 2 * C)
        rhs = jnp.concatenate(
            [w_ref[t, 1 - i : 3 - i, c].reshape(2 * C, C) for i in range(ROWS) for c in range(3)],
            axis=-1,
        )
        y = jnp.dot(lhs, rhs, preferred_element_type=F32)
        if t == 0:
            acc[...] = y
        else:
            acc[...] += y
    for i in range(ROWS):
        part_ref[i] = summed(acc[:, i * 3 * C : (i + 1) * 3 * C])


def outer_rows(edges, w_ref, part_ref):
    out = []
    for i in range(ROWS):
        lhs = jnp.concatenate([edges[i, t : t + 4] for t in range(3)], axis=-1)
        rhs = jnp.concatenate(
            [w_ref[:, 2 * i, c].reshape(3 * C, C) for c in range(3)], axis=-1
        )
        y = jnp.dot(lhs.reshape(4 * WIDE, 3 * C), rhs, preferred_element_type=F32)
        out.append(part_ref[i] + summed(y))
    return out


def summed(y):
    n = y.shape[0]
    return (
        pltpu.roll(y[:, :C], 1, 0) + y[:, C : 2 * C] + pltpu.roll(y[:, 2 * C :], n - 1, 0)
    )


def windows(v):
    edge = jnp.zeros((v.shape[0], 2, C), F32)
    v = jnp.concatenate([edge, v.astype(F32), edge], axis=1)
    return [v[:, q * COLS : q * COLS + WIDE].astype(BF) for q in range(4)]


def pieces_kernel(at_ref, v_ref, own_ref, near_ref, far_ref, held):
    q = at_ref[0]
    for i, window in enumerate(windows(v_ref[0])):
        held[i] = window
    own_ref[...] = held[q]
    near_ref[...] = held[q ^ 1]
    far_ref[0] = held[q ^ 2]
    far_ref[1] = held[q ^ 3]


def caches_kernel(at_ref, first_ref, second_ref, out_ref, held):
    for n, ref in enumerate((first_ref, second_ref)):
        for f in range(2):
            for i, window in enumerate(windows(ref[f])):
                held[i] = window
            out_ref[2 * n + f] = held[at_ref[0]]


def relay_kernel(near_ref, yo_ref, out_ref):
    out_ref[0] = near_ref[...]
    out_ref[1] = yo_ref[1]


def edges_kernel(at_ref, own_ref, yo_ref, co_ref, c_ref, a_ref, b_ref):
    odd = at_ref[1]
    refs = (own_ref, co_ref.at[0], yo_ref.at[0], co_ref.at[1], c_ref.at[0], c_ref.at[1])
    for k, ref in enumerate(refs):
        top, bottom = ref[0], ref[1]
        a_ref[k] = jnp.where(odd == 0, bottom, top)
        b_ref[k] = jnp.where(odd == 0, top, bottom)


def first_inner_kernel(at_ref, p_ref, yo_ref, co_ref, c_ref, g_ref, w_ref, part_ref, frames, acc):
    q = at_ref[0]
    frames[0:2] = c_ref[0:2]
    gain = g_ref[...]
    for k, own in enumerate((p_ref[...], co_ref[0], yo_ref[0], co_ref[1])):
        frames[2 + (q ^ k)] = silu(norm(own.astype(F32), gain)).astype(BF)
    inner_rows(frames, w_ref, acc, part_ref)


def first_outer_kernel(
    at_ref, part_ref, a_ref, b_ref, c_ref, g1_ref, g2_ref, w_ref,
    out_ref, out_a, out_b, edges,
):
    q, odd = at_ref[0], at_ref[1]
    for at_row, rows in ((1 - odd, a_ref), (odd, b_ref)):
        edges[at_row, 0:2] = rows[4:6]
        for k in range(4):
            v = rows[k].astype(F32)
            edges[at_row, 2 + (q ^ k)] = silu(norm(v, g1_ref[...])).astype(BF)
    place = lax.broadcasted_iota(jnp.int32, (WIDE, 1), 0)
    column = place + COLS * q - 2
    valid = (column >= 0) & (column < 4 * COLS) & (place > 0) & (place < WIDE - 1)
    rows = []
    for i, y in enumerate(outer_rows(edges, w_ref, part_ref)):
        h = silu(norm(y, g2_ref[...])).reshape(4, WIDE, C)
        h = jnp.where(valid[None], h, 0.0)
        out_ref[:, i] = h.astype(BF)
        rows.append(h)
    out_a[0:4] = jnp.where(odd == 0, rows[1], rows[0]).astype(BF)
    out_b[0:4] = jnp.where(odd == 0, rows[0], rows[1]).astype(BF)
    for f in range(2):
        out_a[4 + f] = jnp.where(odd == 0, c_ref[2 + f, 1], c_ref[2 + f, 0])
        out_b[4 + f] = jnp.where(odd == 0, c_ref[2 + f, 0], c_ref[2 + f, 1])


def second_inner_kernel(h_ref, c_ref, w_ref, part_ref, frames, acc):
    frames[0:2] = c_ref[2:4]
    frames[2:6] = h_ref[...]
    inner_rows(frames, w_ref, acc, part_ref)


def second_outer_kernel(
    at_ref, part_ref, a_ref, b_ref, p_ref, yo_ref, co_ref, g_ref, w_ref,
    n0, n1, n2, n3, r0, r1, r23, edges, sums, kept,
):
    q, odd, y = at_ref[0], at_ref[1], at_ref[2]
    for at_row, rows in ((1 - odd, a_ref), (odd, b_ref)):
        edges[at_row, 0:2] = rows[4:6]
        edges[at_row, 2:6] = rows[0:4]
    for i, v in enumerate(outer_rows(edges, w_ref, part_ref)):
        sums[:, i] = v.reshape(4, WIDE, C)
    span = ROWS * WIDE
    for k, latent in enumerate((p_ref[...], co_ref[0], yo_ref[0], co_ref[1])):
        f = q ^ k
        total = (sums[f] + latent.astype(F32)).reshape(span, C)
        total = pltpu.roll(total, span - 2, 0)
        kept[f] = jnp.concatenate([total[0:COLS], total[WIDE : WIDE + COLS]], axis=0)
    for k, n_ref in enumerate((n0, n1, n2, n3)):
        n_ref[...] = norm(kept[y ^ k], g_ref[...]).astype(BF)
    r0[...] = kept[q]
    r1[...] = kept[q ^ 1]
    r23[:SLICE] = kept[q ^ 2]
    r23[SLICE:] = kept[q ^ 3]


SCALAR = pl.BlockSpec(memory_space=pltpu.SMEM)
NEAR = pl.BlockSpec(memory_space=pltpu.VMEM)
PARAMS = pltpu.CompilerParams(vmem_limit_bytes=24 * 1024 * 1024)


def cost(flops, moved):
    return pl.CostEstimate(flops=flops, bytes_accessed=moved, transcendentals=0)


FRAMES = pltpu.VMEM((6, ROWS, WIDE, C), BF)
EDGES = pltpu.VMEM((2, 6, WIDE, C), BF)
ACC = pltpu.VMEM((4 * WIDE, ROWS * 3 * C), F32)
PART = jax.ShapeDtypeStruct((ROWS, 4 * WIDE, C), F32)
EDGE = jax.ShapeDtypeStruct((6, WIDE, C), BF)
HIDDEN = jax.ShapeDtypeStruct((4, ROWS, WIDE, C), BF)
UNIT = 2 * 4 * WIDE * 3 * C * 3 * C


def conv_call(kernel, args, scalars, out_shape, scratch, share, name):
    return pl.pallas_call(
        kernel,
        out_shape=out_shape,
        in_specs=[SCALAR] * scalars + [NEAR] * (len(args) - scalars),
        out_specs=jax.tree.map(lambda _: NEAR, out_shape),
        scratch_shapes=scratch,
        compiler_params=PARAMS,
        cost_estimate=cost(share * UNIT, 6_000_000),
        name=name,
    )(*args)


def project(raw, wq_ref, wkv_ref):
    queries = jnp.dot(raw, wq_ref[...], preferred_element_type=F32).astype(BF)
    queries = lax.dot_general(
        queries, wkv_ref[:, :C], (((1,), (1,)), ((), ())), preferred_element_type=F32
    )
    return (queries * SCALE).astype(BF)


def score(queries, keys):
    return lax.dot_general(queries, keys, (((1,), (1,)), ((), ())), preferred_element_type=F32)


def sweep(queries, keys, acc, state):
    rows = queries.shape[0]
    if state is None:
        peak = jnp.full((rows, 1), -1e30, F32)
        total = jnp.zeros((rows, 1), F32)
        acc[...] = jnp.zeros((rows, C), F32)
    else:
        peak, total = state
    scores = score(queries, keys[0][...])
    for i, block in enumerate(keys):
        following = score(queries, keys[i + 1][...]) if i + 1 < len(keys) else None
        risen = jnp.maximum(peak, jnp.max(scores, axis=1, keepdims=True))
        share = jnp.exp2(peak - risen)
        e = jnp.exp2(scores - risen)
        total = total * share + jnp.sum(e, axis=1, keepdims=True)
        acc[...] = acc[...] * share + jnp.dot(
            e.astype(BF), block[...], preferred_element_type=F32
        )
        peak, scores = risen, following
    return peak, total


def noted(peak, total):
    rows = peak.shape[0]
    return jnp.concatenate(
        [jnp.broadcast_to(peak, (rows, 128)), jnp.broadcast_to(total, (rows, 128))], axis=1
    )


def recalled(stats):
    return (
        jnp.max(stats[:, :128], axis=1, keepdims=True),
        jnp.max(stats[:, 128:], axis=1, keepdims=True),
    )


def packed(peak, total, weighted):
    lane = lax.broadcasted_iota(jnp.int32, (peak.shape[0], 128), 1)
    level = peak + jnp.log2(total)
    first = level.astype(BF).astype(F32)
    second = (level - first).astype(BF).astype(F32)
    third = level - first - second
    side = jnp.where(
        lane == 0, first, jnp.where(lane == 1, second, jnp.where(lane == 2, third, 0.0))
    )
    return jnp.concatenate([(weighted / total).astype(BF), side.astype(BF)], axis=1)


def attend_near_kernel(qa, qb, k0, k1, k2, k3, wq, wkv, out, stats):
    queries = project(jnp.concatenate([qa[...], qb[...]], axis=0), wq, wkv)
    stats[...] = noted(*sweep(queries, (k0, k1, k2, k3), out, None))


def attend_far_kernel(qa, qb, weighted, stats, k0, k1, wq, wkv, out_a, out_b, acc):
    acc[...] = weighted[...]
    queries = project(jnp.concatenate([qa[...], qb[...]], axis=0), wq, wkv)
    peak, total = sweep(queries, (k0, k1), acc, recalled(stats))
    result = packed(peak, total, acc[...])
    out_a[...] = result[:BLOCK]
    out_b[...] = result[BLOCK:]


def attend_all_kernel(q, k0, k1, k2, k3, k4, k5, k6, k7, wq, wkv, out, acc):
    queries = project(q[...], wq, wkv)
    peak, total = sweep(queries, (k0, k1, k2, k3, k4, k5, k6, k7), acc, None)
    out[...] = packed(peak, total, acc[...])


def attend_own_kernel(q, k0, k1, wq, wkv, out, stats):
    queries = project(q[...], wq, wkv)
    stats[...] = noted(*sweep(queries, (k0, k1), out, None))


def attend_more_kernel(qa, qb, weighted, before, k0, k1, wq, wkv, out, stats):
    out[...] = weighted[...]
    queries = project(jnp.concatenate([qa[...], qb[...]], axis=0), wq, wkv)
    stats[...] = noted(*sweep(queries, (k0, k1), out, recalled(before)))


def attend_rest_kernel(q, weighted, stats, k0, k1, k2, k3, k4, k5, wq, wkv, out, acc):
    acc[...] = weighted[...]
    queries = project(q[...], wq, wkv)
    peak, total = sweep(queries, (k0, k1, k2, k3, k4, k5), acc, recalled(stats))
    out[...] = packed(peak, total, acc[...])


def attend(kernel, first, keys, weights, out_shape, scratch, flops, name):
    args = list(first) + list(keys) + list(weights)
    return pl.pallas_call(
        kernel,
        out_shape=out_shape,
        in_specs=[NEAR] * len(args),
        out_specs=[NEAR] * len(out_shape),
        scratch_shapes=scratch,
        compiler_params=PARAMS,
        cost_estimate=cost(flops // 8, 2 * BLOCK * C),
        name=name,
    )(*args)


def levels_of(parts):
    return [jnp.sum(p[:, C:].astype(F32), axis=1, keepdims=True) for p in parts]


def merge_first_kernel(p0, p1, out, stats):
    levels = levels_of((p0, p1))
    peak = jnp.maximum(*levels)
    shares = [jnp.exp2(level - peak) for level in levels]
    out[...] = p0[:, :C].astype(F32) * shares[0] + p1[:, :C].astype(F32) * shares[1]
    stats[...] = noted(peak, shares[0] + shares[1])


def merge_first_call(own, across):
    return pl.pallas_call(
        merge_first_kernel,
        in_specs=[NEAR] * 2,
        out_specs=[NEAR] * 2,
        out_shape=[
            jax.ShapeDtypeStruct((BLOCK, C), F32),
            jax.ShapeDtypeStruct((BLOCK, 256), F32),
        ],
        compiler_params=PARAMS,
        name="merge_first",
    )(own, across)


def merge_kernel(at_ref, weighted, stats, p2, p3, wkv_ref, out_a, out_b):
    parts = (p2, p3)
    begun, total = recalled(stats)
    levels = levels_of(parts)
    peak = jnp.maximum(begun, jnp.maximum(*levels))
    share = jnp.exp2(begun - peak)
    mixed, total = weighted[...] * share, total * share
    for part, level in zip(parts, levels):
        share = jnp.exp2(level - peak)
        mixed += part[:, :C].astype(F32) * share
        total += share
    mixed = mixed / total
    y = jnp.dot(mixed.astype(BF), wkv_ref[:, C:], preferred_element_type=F32)
    even = jnp.concatenate([y[:SLICE], y[2 * SLICE : 3 * SLICE]], axis=0)
    odd = jnp.concatenate([y[SLICE : 2 * SLICE], y[3 * SLICE :]], axis=0)
    core = at_ref[3]
    out_a[...] = jnp.where(core == 0, even, odd).astype(BF)
    out_b[...] = jnp.where(core == 0, odd, even).astype(BF)


def merge_call(at, parts, wkv):
    return pl.pallas_call(
        merge_kernel,
        in_specs=[SCALAR] + [NEAR] * 5,
        out_specs=[NEAR] * 2,
        out_shape=[jax.ShapeDtypeStruct((HALF, C), BF)] * 2,
        compiler_params=PARAMS,
        name="merge",
    )(at, *parts, wkv)


def final_kernel(at_ref, a_ref, b_ref, r0, ry, rc, wo_ref, out_ref, parts):
    frame, low = at_ref[0], at_ref[4]
    ya = jnp.dot(a_ref[...], wo_ref[...], preferred_element_type=F32)
    yb = jnp.dot(b_ref[...], wo_ref[...], preferred_element_type=F32)
    even, odd = jnp.where(low == 0, ya, yb), jnp.where(low == 0, yb, ya)
    parts[0] = even[:SLICE] + r0[...]
    parts[1] = odd[:SLICE] + rc[:SLICE]
    parts[2] = even[SLICE:] + ry[:SLICE]
    parts[3] = odd[SLICE:] + rc[SLICE:]
    for q in range(4):
        part = parts[frame ^ q]
        out_ref[0, 0, q * COLS : (q + 1) * COLS] = part[:COLS]
        out_ref[0, 1, q * COLS : (q + 1) * COLS] = part[COLS:]


def final_call(at, a, b, r0, ry, rc, wo):
    return pl.pallas_call(
        final_kernel,
        in_specs=[SCALAR] + [NEAR] * 6,
        out_specs=NEAR,
        out_shape=jax.ShapeDtypeStruct((1, ROWS, 4 * COLS, C), F32),
        scratch_shapes=[pltpu.VMEM((4, SLICE, C), F32)],
        compiler_params=PARAMS,
        name="final",
    )(at, a, b, r0, ry, rc, wo)


def shards(
    latent, cache_first, cache_second, gain_first, conv_first, gain_second, conv_second,
    gain_attention, query_weight, keyvalue_weight, out_weight,
):
    low, high, core = (lax.axis_index(a) for a in ("yl", "yh", "c"))
    member = high * 2 + core
    odd = lax.axis_index("z") % 2
    at = jnp.stack([member, odd, high * 2 + low, core, low]).astype(jnp.int32)

    both = jax.ShapeDtypeStruct((ROWS, WIDE, C), BF)
    two = jax.ShapeDtypeStruct((2, ROWS, WIDE, C), BF)
    held = [pltpu.VMEM((4, ROWS, WIDE, C), BF)]
    pieces, near, far = conv_call(
        pieces_kernel, (at, latent), 1, [both, both, two], held, 0, "pieces"
    )
    yo = send(far, ("yh",), other("yh"))
    caches = conv_call(
        caches_kernel, (at, cache_first, cache_second), 1, HIDDEN, held, 0, "caches"
    )
    near, caches = lax.optimization_barrier((near, caches))
    co = conv_call(relay_kernel, (near, yo), 0, two, [], 0, "relay")
    co = send(co, ("c",), other("c"))

    a, b = conv_call(edges_kernel, (at, pieces, yo, co, caches), 1, [EDGE, EDGE], [], 0, "edges")
    a = send(a, AXES, row_swap(False))
    b = send(b, AXES, row_swap(True))
    gain1, gain2, gain3 = gain_first, gain_second, gain_attention
    part = conv_call(
        first_inner_kernel, (at, pieces, yo, co, caches, gain1, conv_first), 1, PART,
        [FRAMES, ACC], 6, "first_inner",
    )
    hidden, ha, hb = conv_call(
        first_outer_kernel, (at, part, a, b, caches, gain1, gain2, conv_first), 1,
        [HIDDEN, EDGE, EDGE], [EDGES], 2, "first_outer",
    )
    ha = send(ha, AXES, row_swap(False))
    hb = send(hb, AXES, row_swap(True))
    part = conv_call(
        second_inner_kernel, (hidden, caches, conv_second), 0, PART, [FRAMES, ACC], 6,
        "second_inner",
    )
    slice_of = lambda n, kind: jax.ShapeDtypeStruct((n * SLICE, C), kind)
    n0, n1, n2, n3, r0, r1, r23 = conv_call(
        second_outer_kernel,
        (at, part, ha, hb, pieces, yo, co, gain3, conv_second), 1,
        [slice_of(1, BF)] * 4 + [slice_of(1, F32)] * 2 + [slice_of(2, F32)],
        [EDGES, pltpu.VMEM((4, ROWS, WIDE, C), F32), pltpu.VMEM((4, SLICE, C), F32)], 2,
        "second_outer",
    )

    group = ("yl", "yh")
    block = jnp.concatenate([n0] + [send(n, group, to_plane(k + 1)) for k, n in enumerate((n1, n2, n3))])
    lines = ("x", "z", "c")
    cross = lambda v: send(v, ("c",), other("c"))
    keyed = lambda v, turn: send(v, lines, line_swap(turn, True))
    asked = lambda v, turn: send(v, lines, line_swap(turn, False))
    p0 = block
    a0, b0 = keyed(p0, False), keyed(p0, True)
    qa, qb = asked(p0, False), asked(p0, True)
    p1 = cross(p0)
    ab, qo = keyed(a0, True), asked(qb, False)
    a1, b1 = cross(qa), cross(qb)
    weights = (query_weight, keyvalue_weight)

    near_keys = [p0, p1, a0, b0]
    unit = 4 * BLOCK * BLOCK * C
    wide = jax.ShapeDtypeStruct((BLOCK, C + 128), BF)
    begun = lambda n: [
        jax.ShapeDtypeStruct((n * BLOCK, C), F32),
        jax.ShapeDtypeStruct((n * BLOCK, 256), F32),
    ]
    after = lambda v, mark: lax.optimization_barrier((v, mark))[0]
    own_weighted, own_stats = attend(
        attend_own_kernel, [p0], [p0, p1], weights, begun(1), [], 2 * unit, "attend_own"
    )
    weighted, stats = attend(
        attend_near_kernel, [after(qa, own_stats), qb], near_keys, weights, begun(2), [], 8 * unit, "attend_near"
    )
    ba = cross(after(qo, stats))
    ry = send(after(r23, stats), ("yh",), other("yh"))
    weighted, stats = attend(
        attend_more_kernel, [after(qa, stats), qb, weighted, stats], [a1, b1], weights, begun(2),
        [], 4 * unit, "attend_more",
    )
    (to,) = attend(
        attend_all_kernel, [after(qo, stats)], near_keys + [a1, b1, ab, ba], weights, [wide],
        [pltpu.VMEM((BLOCK, C), F32)], 8 * unit, "attend_across",
    )
    sa, sb = attend(
        attend_far_kernel, [after(qa, (to, ry)), qb, weighted, stats], [ab, ba], weights,
        [wide] * 2, [pltpu.VMEM((2 * BLOCK, C), F32)], 4 * unit, "attend_far",
    )
    (own,) = attend(
        attend_rest_kernel, [after(p0, sa), own_weighted, own_stats],
        [a0, b0, a1, b1, ab, ba], weights, [wide],
        [pltpu.VMEM((BLOCK, C), F32)], 6 * unit, "attend_rest",
    )
    to = send(to, lines, line_across)
    rc_from = after(ry, sa)
    sa, sb = asked(sa, False), asked(sb, True)
    rc = cross(jnp.concatenate([r1, rc_from[SLICE:]]))
    to_a, to_b = merge_call(at, (*merge_first_call(own, to), sa, sb), keyvalue_weight)
    home = ("yl", "c")
    to_a, to_b = send(to_a, home, to_home(0)), send(to_b, home, to_home(1))
    return final_call(at, to_a, to_b, r0, ry, rc, out_weight)


def solution(mesh):
    fine = Mesh(mesh.devices.reshape([SIZES[a] for a in AXES]), AXES)
    frames, rows = ("yh", "c"), ("x", "yl", "z")
    in_specs = (P(frames, rows), P(None, rows), P(None, rows)) + (P(),) * 8
    return jax.shard_map(
        shards, mesh=fine, in_specs=in_specs, out_specs=P(frames, rows), check_vma=False
    )
```

```python
import functools
import math

import jax
import jax.numpy as jnp
from jax import lax
from jax.experimental import pallas as pl
from jax.experimental.pallas import tpu as pltpu
from jax.sharding import Mesh
from jax.sharding import PartitionSpec as P

C = 384
COLS = 60
WIDE = 64
ROWS = 2
SLICE = ROWS * COLS
BLOCK = 4 * SLICE
HALF = BLOCK // 2
AXES = ("x", "yl", "z", "yh", "c")
SIZES = {"x": 4, "yl": 2, "z": 4, "yh": 2, "c": 2}
BF = jnp.bfloat16
F32 = jnp.float32
SCALE = math.log2(math.e) / math.sqrt(C)


def routes(axes, target):
    sizes = [SIZES[a] for a in axes]
    total = math.prod(sizes)
    pairs = []
    for source in range(total):
        rest, where = source, {}
        for a, n in zip(reversed(axes), reversed(sizes)):
            where[a] = rest % n
            rest //= n
        there = target(dict(where))
        if there is None:
            continue
        index = 0
        for a, n in zip(axes, sizes):
            index = index * n + there[a] % n
        pairs.append((source, index))
    return pairs


def send(value, axes, target):
    return lax.ppermute(value, axes, routes(axes, target))


def row_swap(odd):
    def target(w):
        row = (w["x"] * 2 + w["yl"]) * 4 + w["z"]
        row = ((row + 1) ^ 1) - 1 if odd else row ^ 1
        if row < 0 or row > 31:
            return None
        return {"x": row // 8, "yl": row // 4 % 2, "z": row % 4, "yh": w["yh"], "c": w["c"]}

    return target


def other(axis):
    return lambda w: {axis: 1 - w[axis]}


def to_plane(k):
    def target(w):
        frame = (w["yh"] * 2 + w["yl"]) ^ k
        return {"yh": frame // 2, "yl": frame % 2}

    return target


def line_swap(odd, key_line):
    def target(w):
        axis = "x" if (w["c"] == 0) == key_line else "z"
        w[axis] = (w[axis] + 1) % 4 ^ 1
        w[axis] = (w[axis] - 1) % 4
        return w

    def even(w):
        axis = "x" if (w["c"] == 0) == key_line else "z"
        w[axis] ^= 1
        return w

    return target if odd else even


def line_across(w):
    axis = "z" if w["c"] == 0 else "x"
    w[axis] = (w[axis] + 2) % 4
    return w


def to_home(j):
    return lambda w: {"yl": w["yl"] ^ w["c"] ^ j, "c": w["yl"]}


def norm(v, gain):
    return v * lax.rsqrt(jnp.mean(v * v, axis=-1, keepdims=True) + 1e-06) * gain


def silu(v):
    return v / (1.0 + jnp.exp(-v))


def inner_rows(frames, w_ref, acc, part_ref):
    for t in range(3):
        xs = frames[t : t + 4]
        lhs = jnp.concatenate([xs[:, 0], xs[:, 1]], axis=-1).reshape(4 * WIDE, 2 * C)
        rhs = jnp.concatenate(
            [w_ref[t, 1 - i : 3 - i, c].reshape(2 * C, C) for i in range(ROWS) for c in range(3)],
            axis=-1,
        )
        y = jnp.dot(lhs, rhs, preferred_element_type=F32)
        if t == 0:
            acc[...] = y
        else:
            acc[...] += y
    for i in range(ROWS):
        part_ref[i] = summed(acc[:, i * 3 * C : (i + 1) * 3 * C])


def outer_rows(edges, w_ref, part_ref):
    out = []
    for i in range(ROWS):
        lhs = jnp.concatenate([edges[i, t : t + 4] for t in range(3)], axis=-1)
        rhs = jnp.concatenate(
            [w_ref[:, 2 * i, c].reshape(3 * C, C) for c in range(3)], axis=-1
        )
        y = jnp.dot(lhs.reshape(4 * WIDE, 3 * C), rhs, preferred_element_type=F32)
        out.append(part_ref[i] + summed(y))
    return out


def summed(y):
    n = y.shape[0]
    return (
        pltpu.roll(y[:, :C], 1, 0) + y[:, C : 2 * C] + pltpu.roll(y[:, 2 * C :], n - 1, 0)
    )


def windows(v):
    edge = jnp.zeros((v.shape[0], 2, C), F32)
    v = jnp.concatenate([edge, v.astype(F32), edge], axis=1)
    return [v[:, q * COLS : q * COLS + WIDE].astype(BF) for q in range(4)]


def pieces_kernel(at_ref, v_ref, own_ref, near_ref, far_ref, held):
    q = at_ref[0]
    for i, window in enumerate(windows(v_ref[0])):
        held[i] = window
    own_ref[...] = held[q]
    near_ref[...] = held[q ^ 1]
    far_ref[0] = held[q ^ 2]
    far_ref[1] = held[q ^ 3]


def caches_kernel(at_ref, first_ref, second_ref, out_ref, held):
    for n, ref in enumerate((first_ref, second_ref)):
        for f in range(2):
            for i, window in enumerate(windows(ref[f])):
                held[i] = window
            out_ref[2 * n + f] = held[at_ref[0]]


def relay_kernel(near_ref, yo_ref, out_ref):
    out_ref[0] = near_ref[...]
    out_ref[1] = yo_ref[1]


def edges_kernel(at_ref, own_ref, yo_ref, co_ref, c_ref, a_ref, b_ref):
    odd = at_ref[1]
    refs = (own_ref, co_ref.at[0], yo_ref.at[0], co_ref.at[1], c_ref.at[0], c_ref.at[1])
    for k, ref in enumerate(refs):
        top, bottom = ref[0], ref[1]
        a_ref[k] = jnp.where(odd == 0, bottom, top)
        b_ref[k] = jnp.where(odd == 0, top, bottom)


def first_inner_kernel(at_ref, p_ref, yo_ref, co_ref, c_ref, g_ref, w_ref, part_ref, frames, acc):
    q = at_ref[0]
    frames[0:2] = c_ref[0:2]
    gain = g_ref[...]
    for k, own in enumerate((p_ref[...], co_ref[0], yo_ref[0], co_ref[1])):
        frames[2 + (q ^ k)] = silu(norm(own.astype(F32), gain)).astype(BF)
    inner_rows(frames, w_ref, acc, part_ref)


def first_outer_kernel(
    at_ref, part_ref, a_ref, b_ref, c_ref, g1_ref, g2_ref, w_ref,
    out_ref, out_a, out_b, edges,
):
    q, odd = at_ref[0], at_ref[1]
    for at_row, rows in ((1 - odd, a_ref), (odd, b_ref)):
        edges[at_row, 0:2] = rows[4:6]
        for k in range(4):
            v = rows[k].astype(F32)
            edges[at_row, 2 + (q ^ k)] = silu(norm(v, g1_ref[...])).astype(BF)
    place = lax.broadcasted_iota(jnp.int32, (WIDE, 1), 0)
    column = place + COLS * q - 2
    valid = (column >= 0) & (column < 4 * COLS) & (place > 0) & (place < WIDE - 1)
    rows = []
    for i, y in enumerate(outer_rows(edges, w_ref, part_ref)):
        h = silu(norm(y, g2_ref[...])).reshape(4, WIDE, C)
        h = jnp.where(valid[None], h, 0.0)
        out_ref[:, i] = h.astype(BF)
        rows.append(h)
    out_a[0:4] = jnp.where(odd == 0, rows[1], rows[0]).astype(BF)
    out_b[0:4] = jnp.where(odd == 0, rows[0], rows[1]).astype(BF)
    for f in range(2):
        out_a[4 + f] = jnp.where(odd == 0, c_ref[2 + f, 1], c_ref[2 + f, 0])
        out_b[4 + f] = jnp.where(odd == 0, c_ref[2 + f, 0], c_ref[2 + f, 1])


def second_inner_kernel(h_ref, c_ref, w_ref, part_ref, frames, acc):
    frames[0:2] = c_ref[2:4]
    frames[2:6] = h_ref[...]
    inner_rows(frames, w_ref, acc, part_ref)


def second_outer_kernel(
    at_ref, part_ref, a_ref, b_ref, p_ref, yo_ref, co_ref, g_ref, w_ref,
    n0, n1, n2, n3, r0, r1, r23, edges, sums, kept,
):
    q, odd, y = at_ref[0], at_ref[1], at_ref[2]
    for at_row, rows in ((1 - odd, a_ref), (odd, b_ref)):
        edges[at_row, 0:2] = rows[4:6]
        edges[at_row, 2:6] = rows[0:4]
    for i, v in enumerate(outer_rows(edges, w_ref, part_ref)):
        sums[:, i] = v.reshape(4, WIDE, C)
    span = ROWS * WIDE
    for k, latent in enumerate((p_ref[...], co_ref[0], yo_ref[0], co_ref[1])):
        f = q ^ k
        total = (sums[f] + latent.astype(F32)).reshape(span, C)
        total = pltpu.roll(total, span - 2, 0)
        kept[f] = jnp.concatenate([total[0:COLS], total[WIDE : WIDE + COLS]], axis=0)
    for k, n_ref in enumerate((n0, n1, n2, n3)):
        n_ref[...] = norm(kept[y ^ k], g_ref[...]).astype(BF)
    r0[...] = kept[q]
    r1[...] = kept[q ^ 1]
    r23[:SLICE] = kept[q ^ 2]
    r23[SLICE:] = kept[q ^ 3]


SCALAR = pl.BlockSpec(memory_space=pltpu.SMEM)
NEAR = pl.BlockSpec(memory_space=pltpu.VMEM)
PARAMS = pltpu.CompilerParams(vmem_limit_bytes=24 * 1024 * 1024)


def cost(flops, moved):
    return pl.CostEstimate(flops=flops, bytes_accessed=moved, transcendentals=0)


FRAMES = pltpu.VMEM((6, ROWS, WIDE, C), BF)
EDGES = pltpu.VMEM((2, 6, WIDE, C), BF)
ACC = pltpu.VMEM((4 * WIDE, ROWS * 3 * C), F32)
PART = jax.ShapeDtypeStruct((ROWS, 4 * WIDE, C), F32)
EDGE = jax.ShapeDtypeStruct((6, WIDE, C), BF)
HIDDEN = jax.ShapeDtypeStruct((4, ROWS, WIDE, C), BF)
UNIT = 2 * 4 * WIDE * 3 * C * 3 * C


def conv_call(kernel, args, scalars, out_shape, scratch, share, name):
    return pl.pallas_call(
        kernel,
        out_shape=out_shape,
        in_specs=[SCALAR] * scalars + [NEAR] * (len(args) - scalars),
        out_specs=jax.tree.map(lambda _: NEAR, out_shape),
        scratch_shapes=scratch,
        compiler_params=PARAMS,
        cost_estimate=cost(share * UNIT, 6_000_000),
        name=name,
    )(*args)


def project(raw, wq_ref, wkv_ref):
    queries = jnp.dot(raw, wq_ref[...], preferred_element_type=F32).astype(BF)
    queries = lax.dot_general(
        queries, wkv_ref[:, :C], (((1,), (1,)), ((), ())), preferred_element_type=F32
    )
    return (queries * SCALE).astype(BF)


def score(queries, keys):
    return lax.dot_general(queries, keys, (((1,), (1,)), ((), ())), preferred_element_type=F32)


def sweep(queries, keys, acc, state):
    rows = queries.shape[0]
    if state is None:
        peak = jnp.full((rows, 1), -1e30, F32)
        total = jnp.zeros((rows, 1), F32)
        acc[...] = jnp.zeros((rows, C), F32)
    else:
        peak, total = state
    scores = score(queries, keys[0][...])
    for i, block in enumerate(keys):
        following = score(queries, keys[i + 1][...]) if i + 1 < len(keys) else None
        risen = jnp.maximum(peak, jnp.max(scores, axis=1, keepdims=True))
        share = jnp.exp2(peak - risen)
        e = jnp.exp2(scores - risen)
        total = total * share + jnp.sum(e, axis=1, keepdims=True)
        acc[...] = acc[...] * share + jnp.dot(
            e.astype(BF), block[...], preferred_element_type=F32
        )
        peak, scores = risen, following
    return peak, total


def noted(peak, total):
    rows = peak.shape[0]
    return jnp.concatenate(
        [jnp.broadcast_to(peak, (rows, 128)), jnp.broadcast_to(total, (rows, 128))], axis=1
    )


def recalled(stats):
    return (
        jnp.max(stats[:, :128], axis=1, keepdims=True),
        jnp.max(stats[:, 128:], axis=1, keepdims=True),
    )


def diagonal():
    row = lax.broadcasted_iota(jnp.int32, (HALF, C), 0)
    return row == lax.broadcasted_iota(jnp.int32, (HALF, C), 1)


def packed(peak, total, weighted):
    level = peak + jnp.log2(total)
    place = lax.broadcasted_iota(jnp.int32, (16, C), 0)
    tail = jnp.zeros((16, C), F32)
    for half in range(2):
        column = level[half * HALF : (half + 1) * HALF]
        line = jnp.sum(jnp.where(diagonal(), column, 0.0), axis=0, keepdims=True)
        first = line.astype(BF).astype(F32)
        second = (line - first).astype(BF).astype(F32)
        for p, piece in enumerate((first, second, line - first - second)):
            tail = jnp.where(place == 2 * p + half, piece, tail)
    return jnp.concatenate([(weighted / total).astype(BF), tail.astype(BF)], axis=0)


def level_of(part):
    tail = part[BLOCK:].astype(F32)
    place = lax.broadcasted_iota(jnp.int32, (16, C), 0)
    columns = []
    for half in range(2):
        line = jnp.sum(jnp.where(place % 2 == half, tail, 0.0), axis=0, keepdims=True)
        columns.append(jnp.sum(jnp.where(diagonal(), line, 0.0), axis=1, keepdims=True))
    return jnp.concatenate(columns, axis=0)


def attend_near_kernel(qa, qb, k0, k1, k2, k3, wq, wkv, out, stats):
    queries = project(jnp.concatenate([qa[...], qb[...]], axis=0), wq, wkv)
    stats[...] = noted(*sweep(queries, (k0, k1, k2, k3), out, None))


def attend_far_kernel(qa, qb, weighted, stats, k0, k1, wq, wkv, out_a, out_b, acc):
    acc[...] = weighted[...]
    queries = project(jnp.concatenate([qa[...], qb[...]], axis=0), wq, wkv)
    peak, total = sweep(queries, (k0, k1), acc, recalled(stats))
    out_a[...] = packed(peak[:BLOCK], total[:BLOCK], acc[:BLOCK])
    out_b[...] = packed(peak[BLOCK:], total[BLOCK:], acc[BLOCK:])


def attend_all_kernel(q, k0, k1, k2, k3, k4, k5, k6, k7, wq, wkv, out, acc):
    queries = project(q[...], wq, wkv)
    peak, total = sweep(queries, (k0, k1, k2, k3, k4, k5, k6, k7), acc, None)
    out[...] = packed(peak, total, acc[...])


def attend_own_kernel(q, k0, k1, wq, wkv, out, stats):
    queries = project(q[...], wq, wkv)
    stats[...] = noted(*sweep(queries, (k0, k1), out, None))


def attend_more_kernel(qa, qb, weighted, before, k0, k1, wq, wkv, out, stats):
    out[...] = weighted[...]
    queries = project(jnp.concatenate([qa[...], qb[...]], axis=0), wq, wkv)
    stats[...] = noted(*sweep(queries, (k0, k1), out, recalled(before)))


def attend_rest_kernel(q, weighted, stats, k0, k1, k2, k3, k4, k5, wq, wkv, out, acc):
    acc[...] = weighted[...]
    queries = project(q[...], wq, wkv)
    peak, total = sweep(queries, (k0, k1, k2, k3, k4, k5), acc, recalled(stats))
    out[...] = packed(peak, total, acc[...])


def attend(kernel, first, keys, weights, out_shape, scratch, flops, name):
    args = list(first) + list(keys) + list(weights)
    return pl.pallas_call(
        kernel,
        out_shape=out_shape,
        in_specs=[NEAR] * len(args),
        out_specs=[NEAR] * len(out_shape),
        scratch_shapes=scratch,
        compiler_params=PARAMS,
        cost_estimate=cost(flops // 8, 2 * BLOCK * C),
        name=name,
    )(*args)


def levels_of(parts):
    return [level_of(p) for p in parts]


def merge_first_kernel(p0, p1, out, stats):
    levels = levels_of((p0, p1))
    peak = jnp.maximum(*levels)
    shares = [jnp.exp2(level - peak) for level in levels]
    out[...] = p0[:BLOCK].astype(F32) * shares[0] + p1[:BLOCK].astype(F32) * shares[1]
    stats[...] = noted(peak, shares[0] + shares[1])


def merge_first_call(own, across):
    return pl.pallas_call(
        merge_first_kernel,
        in_specs=[NEAR] * 2,
        out_specs=[NEAR] * 2,
        out_shape=[
            jax.ShapeDtypeStruct((BLOCK, C), F32),
            jax.ShapeDtypeStruct((BLOCK, 256), F32),
        ],
        compiler_params=PARAMS,
        name="merge_first",
    )(own, across)


def merge_kernel(at_ref, weighted, stats, p2, p3, wkv_ref, out_a, out_b):
    parts = (p2, p3)
    begun, total = recalled(stats)
    levels = levels_of(parts)
    peak = jnp.maximum(begun, jnp.maximum(*levels))
    share = jnp.exp2(begun - peak)
    mixed, total = weighted[...] * share, total * share
    for part, level in zip(parts, levels):
        share = jnp.exp2(level - peak)
        mixed += part[:BLOCK].astype(F32) * share
        total += share
    mixed = mixed / total
    y = jnp.dot(mixed.astype(BF), wkv_ref[:, C:], preferred_element_type=F32)
    even = jnp.concatenate([y[:SLICE], y[2 * SLICE : 3 * SLICE]], axis=0)
    odd = jnp.concatenate([y[SLICE : 2 * SLICE], y[3 * SLICE :]], axis=0)
    core = at_ref[3]
    out_a[...] = jnp.where(core == 0, even, odd).astype(BF)
    out_b[...] = jnp.where(core == 0, odd, even).astype(BF)


def merge_call(at, parts, wkv):
    return pl.pallas_call(
        merge_kernel,
        in_specs=[SCALAR] + [NEAR] * 5,
        out_specs=[NEAR] * 2,
        out_shape=[jax.ShapeDtypeStruct((HALF, C), BF)] * 2,
        compiler_params=PARAMS,
        name="merge",
    )(at, *parts, wkv)


def final_kernel(at_ref, a_ref, b_ref, r0, ry, rc, wo_ref, out_ref, parts):
    frame, low = at_ref[0], at_ref[4]
    ya = jnp.dot(a_ref[...], wo_ref[...], preferred_element_type=F32)
    yb = jnp.dot(b_ref[...], wo_ref[...], preferred_element_type=F32)
    even, odd = jnp.where(low == 0, ya, yb), jnp.where(low == 0, yb, ya)
    parts[0] = even[:SLICE] + r0[...]
    parts[1] = odd[:SLICE] + rc[:SLICE]
    parts[2] = even[SLICE:] + ry[:SLICE]
    parts[3] = odd[SLICE:] + rc[SLICE:]
    for q in range(4):
        part = parts[frame ^ q]
        out_ref[0, 0, q * COLS : (q + 1) * COLS] = part[:COLS]
        out_ref[0, 1, q * COLS : (q + 1) * COLS] = part[COLS:]


def final_call(at, a, b, r0, ry, rc, wo):
    return pl.pallas_call(
        final_kernel,
        in_specs=[SCALAR] + [NEAR] * 6,
        out_specs=NEAR,
        out_shape=jax.ShapeDtypeStruct((1, ROWS, 4 * COLS, C), F32),
        scratch_shapes=[pltpu.VMEM((4, SLICE, C), F32)],
        compiler_params=PARAMS,
        name="final",
    )(at, a, b, r0, ry, rc, wo)


def shards(
    latent, cache_first, cache_second, gain_first, conv_first, gain_second, conv_second,
    gain_attention, query_weight, keyvalue_weight, out_weight,
):
    low, high, core = (lax.axis_index(a) for a in ("yl", "yh", "c"))
    member = high * 2 + core
    odd = lax.axis_index("z") % 2
    at = jnp.stack([member, odd, high * 2 + low, core, low]).astype(jnp.int32)

    both = jax.ShapeDtypeStruct((ROWS, WIDE, C), BF)
    two = jax.ShapeDtypeStruct((2, ROWS, WIDE, C), BF)
    held = [pltpu.VMEM((4, ROWS, WIDE, C), BF)]
    pieces, near, far = conv_call(
        pieces_kernel, (at, latent), 1, [both, both, two], held, 0, "pieces"
    )
    yo = send(far, ("yh",), other("yh"))
    caches = conv_call(
        caches_kernel, (at, cache_first, cache_second), 1, HIDDEN, held, 0, "caches"
    )
    near, caches = lax.optimization_barrier((near, caches))
    co = conv_call(relay_kernel, (near, yo), 0, two, [], 0, "relay")
    co = send(co, ("c",), other("c"))

    a, b = conv_call(edges_kernel, (at, pieces, yo, co, caches), 1, [EDGE, EDGE], [], 0, "edges")
    a = send(a, AXES, row_swap(False))
    b = send(b, AXES, row_swap(True))
    gain1, gain2, gain3 = gain_first, gain_second, gain_attention
    part = conv_call(
        first_inner_kernel, (at, pieces, yo, co, caches, gain1, conv_first), 1, PART,
        [FRAMES, ACC], 6, "first_inner",
    )
    hidden, ha, hb = conv_call(
        first_outer_kernel, (at, part, a, b, caches, gain1, gain2, conv_first), 1,
        [HIDDEN, EDGE, EDGE], [EDGES], 2, "first_outer",
    )
    ha = send(ha, AXES, row_swap(False))
    hb = send(hb, AXES, row_swap(True))
    part = conv_call(
        second_inner_kernel, (hidden, caches, conv_second), 0, PART, [FRAMES, ACC], 6,
        "second_inner",
    )
    slice_of = lambda n, kind: jax.ShapeDtypeStruct((n * SLICE, C), kind)
    n0, n1, n2, n3, r0, r1, r23 = conv_call(
        second_outer_kernel,
        (at, part, ha, hb, pieces, yo, co, gain3, conv_second), 1,
        [slice_of(1, BF)] * 4 + [slice_of(1, F32)] * 2 + [slice_of(2, F32)],
        [EDGES, pltpu.VMEM((4, ROWS, WIDE, C), F32), pltpu.VMEM((4, SLICE, C), F32)], 2,
        "second_outer",
    )

    group = ("yl", "yh")
    block = jnp.concatenate([n0] + [send(n, group, to_plane(k + 1)) for k, n in enumerate((n1, n2, n3))])
    lines = ("x", "z", "c")
    cross = lambda v: send(v, ("c",), other("c"))
    keyed = lambda v, turn: send(v, lines, line_swap(turn, True))
    asked = lambda v, turn: send(v, lines, line_swap(turn, False))
    p0 = block
    a0, b0 = keyed(p0, False), keyed(p0, True)
    qa, qb = asked(p0, False), asked(p0, True)
    p1 = cross(p0)
    ab, qo = keyed(a0, True), asked(qb, False)
    a1, b1 = cross(qa), cross(qb)
    weights = (query_weight, keyvalue_weight)

    near_keys = [p0, p1, a0, b0]
    unit = 4 * BLOCK * BLOCK * C
    wide = jax.ShapeDtypeStruct((BLOCK + 16, C), BF)
    begun = lambda n: [
        jax.ShapeDtypeStruct((n * BLOCK, C), F32),
        jax.ShapeDtypeStruct((n * BLOCK, 256), F32),
    ]
    after = lambda v, mark: lax.optimization_barrier((v, mark))[0]
    own_weighted, own_stats = attend(
        attend_own_kernel, [p0], [p0, p1], weights, begun(1), [], 2 * unit, "attend_own"
    )
    weighted, stats = attend(
        attend_near_kernel, [after(qa, own_stats), qb], near_keys, weights, begun(2), [], 8 * unit, "attend_near"
    )
    ba = cross(after(qo, stats))
    ry = send(after(r23, stats), ("yh",), other("yh"))
    weighted, stats = attend(
        attend_more_kernel, [after(qa, stats), qb, weighted, stats], [a1, b1], weights, begun(2),
        [], 4 * unit, "attend_more",
    )
    (to,) = attend(
        attend_all_kernel, [after(qo, stats)], near_keys + [a1, b1, ab, ba], weights, [wide],
        [pltpu.VMEM((BLOCK, C), F32)], 8 * unit, "attend_across",
    )
    sa, sb = attend(
        attend_far_kernel, [after(qa, (to, ry)), qb, weighted, stats], [ab, ba], weights,
        [wide] * 2, [pltpu.VMEM((2 * BLOCK, C), F32)], 4 * unit, "attend_far",
    )
    (own,) = attend(
        attend_rest_kernel, [after(p0, sa), own_weighted, own_stats],
        [a0, b0, a1, b1, ab, ba], weights, [wide],
        [pltpu.VMEM((BLOCK, C), F32)], 6 * unit, "attend_rest",
    )
    to = send(to, lines, line_across)
    rc_from = after(ry, sa)
    sa, sb = asked(sa, False), asked(sb, True)
    rc = cross(jnp.concatenate([r1, rc_from[SLICE:]]))
    to_a, to_b = merge_call(at, (*merge_first_call(own, to), sa, sb), keyvalue_weight)
    home = ("yl", "c")
    to_a, to_b = send(to_a, home, to_home(0)), send(to_b, home, to_home(1))
    return final_call(at, to_a, to_b, r0, ry, rc, out_weight)


def solution(mesh):
    fine = Mesh(mesh.devices.reshape([SIZES[a] for a in AXES]), AXES)
    frames, rows = ("yh", "c"), ("x", "yl", "z")
    in_specs = (P(frames, rows), P(None, rows), P(None, rows)) + (P(),) * 8
    return jax.shard_map(
        shards, mesh=fine, in_specs=in_specs, out_specs=P(frames, rows), check_vma=False
    )
```

```python
import functools
import math

import jax
import jax.numpy as jnp
from jax import lax
from jax.experimental import pallas as pl
from jax.experimental.pallas import tpu as pltpu
from jax.sharding import Mesh
from jax.sharding import PartitionSpec as P

C = 384
COLS = 60
WIDE = 64
ROWS = 2
SLICE = ROWS * COLS
BLOCK = 4 * SLICE
HALF = BLOCK // 2
AXES = ("x", "yl", "z", "yh", "c")
SIZES = {"x": 4, "yl": 2, "z": 4, "yh": 2, "c": 2}
BF = jnp.bfloat16
F32 = jnp.float32
SCALE = math.log2(math.e) / math.sqrt(C)


def routes(axes, target):
    sizes = [SIZES[a] for a in axes]
    total = math.prod(sizes)
    pairs = []
    for source in range(total):
        rest, where = source, {}
        for a, n in zip(reversed(axes), reversed(sizes)):
            where[a] = rest % n
            rest //= n
        there = target(dict(where))
        if there is None:
            continue
        index = 0
        for a, n in zip(axes, sizes):
            index = index * n + there[a] % n
        pairs.append((source, index))
    return pairs


def send(value, axes, target):
    return lax.ppermute(value, axes, routes(axes, target))


def row_swap(odd):
    def target(w):
        row = (w["x"] * 2 + w["yl"]) * 4 + w["z"]
        row = ((row + 1) ^ 1) - 1 if odd else row ^ 1
        if row < 0 or row > 31:
            return None
        return {"x": row // 8, "yl": row // 4 % 2, "z": row % 4, "yh": w["yh"], "c": w["c"]}

    return target


def other(axis):
    return lambda w: {axis: 1 - w[axis]}


def to_plane(k):
    def target(w):
        frame = (w["yh"] * 2 + w["yl"]) ^ k
        return {"yh": frame // 2, "yl": frame % 2}

    return target


def line_swap(odd, key_line):
    def target(w):
        axis = "x" if (w["c"] == 0) == key_line else "z"
        w[axis] = (w[axis] + 1) % 4 ^ 1
        w[axis] = (w[axis] - 1) % 4
        return w

    def even(w):
        axis = "x" if (w["c"] == 0) == key_line else "z"
        w[axis] ^= 1
        return w

    return target if odd else even


def line_across(w):
    axis = "z" if w["c"] == 0 else "x"
    w[axis] = (w[axis] + 2) % 4
    return w


def to_home(j):
    return lambda w: {"yl": w["yl"] ^ w["c"] ^ j, "c": w["yl"]}


def norm(v, gain):
    return v * lax.rsqrt(jnp.mean(v * v, axis=-1, keepdims=True) + 1e-06) * gain


def silu(v):
    return v / (1.0 + jnp.exp(-v))


def inner_rows(frames, w_ref, acc, part_ref):
    for t in range(3):
        xs = frames[t : t + 4]
        lhs = jnp.concatenate([xs[:, 0], xs[:, 1]], axis=-1).reshape(4 * WIDE, 2 * C)
        rhs = jnp.concatenate(
            [w_ref[t, 1 - i : 3 - i, c].reshape(2 * C, C) for i in range(ROWS) for c in range(3)],
            axis=-1,
        )
        y = jnp.dot(lhs, rhs, preferred_element_type=F32)
        if t == 0:
            acc[...] = y
        else:
            acc[...] += y
    for i in range(ROWS):
        part_ref[i] = summed(acc[:, i * 3 * C : (i + 1) * 3 * C])


def outer_rows(edges, w_ref, part_ref):
    out = []
    for i in range(ROWS):
        lhs = jnp.concatenate([edges[i, t : t + 4] for t in range(3)], axis=-1)
        rhs = jnp.concatenate(
            [w_ref[:, 2 * i, c].reshape(3 * C, C) for c in range(3)], axis=-1
        )
        y = jnp.dot(lhs.reshape(4 * WIDE, 3 * C), rhs, preferred_element_type=F32)
        out.append(part_ref[i] + summed(y))
    return out


def summed(y):
    n = y.shape[0]
    return (
        pltpu.roll(y[:, :C], 1, 0) + y[:, C : 2 * C] + pltpu.roll(y[:, 2 * C :], n - 1, 0)
    )


def windows(v):
    edge = jnp.zeros((v.shape[0], 2, C), F32)
    v = jnp.concatenate([edge, v.astype(F32), edge], axis=1)
    return [v[:, q * COLS : q * COLS + WIDE].astype(BF) for q in range(4)]


def pieces_kernel(at_ref, v_ref, own_ref, near_ref, far_ref, held):
    q = at_ref[0]
    for i, window in enumerate(windows(v_ref[0])):
        held[i] = window
    own_ref[...] = held[q]
    near_ref[...] = held[q ^ 1]
    far_ref[0] = held[q ^ 2]
    far_ref[1] = held[q ^ 3]


def caches_kernel(at_ref, first_ref, second_ref, out_ref, held):
    for n, ref in enumerate((first_ref, second_ref)):
        for f in range(2):
            for i, window in enumerate(windows(ref[f])):
                held[i] = window
            out_ref[2 * n + f] = held[at_ref[0]]


def relay_kernel(near_ref, yo_ref, out_ref):
    out_ref[0] = near_ref[...]
    out_ref[1] = yo_ref[1]


def edges_kernel(at_ref, own_ref, yo_ref, co_ref, c_ref, a_ref, b_ref):
    odd = at_ref[1]
    refs = (own_ref, co_ref.at[0], yo_ref.at[0], co_ref.at[1], c_ref.at[0], c_ref.at[1])
    for k, ref in enumerate(refs):
        top, bottom = ref[0], ref[1]
        a_ref[k] = jnp.where(odd == 0, bottom, top)
        b_ref[k] = jnp.where(odd == 0, top, bottom)


def first_inner_kernel(at_ref, p_ref, yo_ref, co_ref, c_ref, g_ref, w_ref, part_ref, frames, acc):
    q = at_ref[0]
    frames[0:2] = c_ref[0:2]
    gain = g_ref[...]
    for k, own in enumerate((p_ref[...], co_ref[0], yo_ref[0], co_ref[1])):
        frames[2 + (q ^ k)] = silu(norm(own.astype(F32), gain)).astype(BF)
    inner_rows(frames, w_ref, acc, part_ref)


def first_outer_kernel(
    at_ref, part_ref, a_ref, b_ref, c_ref, g1_ref, g2_ref, w_ref,
    out_ref, out_a, out_b, edges,
):
    q, odd = at_ref[0], at_ref[1]
    for at_row, rows in ((1 - odd, a_ref), (odd, b_ref)):
        edges[at_row, 0:2] = rows[4:6]
        for k in range(4):
            v = rows[k].astype(F32)
            edges[at_row, 2 + (q ^ k)] = silu(norm(v, g1_ref[...])).astype(BF)
    place = lax.broadcasted_iota(jnp.int32, (WIDE, 1), 0)
    column = place + COLS * q - 2
    valid = (column >= 0) & (column < 4 * COLS) & (place > 0) & (place < WIDE - 1)
    rows = []
    for i, y in enumerate(outer_rows(edges, w_ref, part_ref)):
        h = silu(norm(y, g2_ref[...])).reshape(4, WIDE, C)
        h = jnp.where(valid[None], h, 0.0)
        out_ref[:, i] = h.astype(BF)
        rows.append(h)
    out_a[0:4] = jnp.where(odd == 0, rows[1], rows[0]).astype(BF)
    out_b[0:4] = jnp.where(odd == 0, rows[0], rows[1]).astype(BF)
    for f in range(2):
        out_a[4 + f] = jnp.where(odd == 0, c_ref[2 + f, 1], c_ref[2 + f, 0])
        out_b[4 + f] = jnp.where(odd == 0, c_ref[2 + f, 0], c_ref[2 + f, 1])


def second_inner_kernel(h_ref, c_ref, w_ref, part_ref, frames, acc):
    frames[0:2] = c_ref[2:4]
    frames[2:6] = h_ref[...]
    inner_rows(frames, w_ref, acc, part_ref)


def second_outer_kernel(
    at_ref, part_ref, a_ref, b_ref, p_ref, yo_ref, co_ref, g_ref, w_ref,
    n0, n1, n2, n3, r0, r1, r23, edges, sums, kept,
):
    q, odd, y = at_ref[0], at_ref[1], at_ref[2]
    for at_row, rows in ((1 - odd, a_ref), (odd, b_ref)):
        edges[at_row, 0:2] = rows[4:6]
        edges[at_row, 2:6] = rows[0:4]
    for i, v in enumerate(outer_rows(edges, w_ref, part_ref)):
        sums[:, i] = v.reshape(4, WIDE, C)
    span = ROWS * WIDE
    for k, latent in enumerate((p_ref[...], co_ref[0], yo_ref[0], co_ref[1])):
        f = q ^ k
        total = (sums[f] + latent.astype(F32)).reshape(span, C)
        total = pltpu.roll(total, span - 2, 0)
        kept[f] = jnp.concatenate([total[0:COLS], total[WIDE : WIDE + COLS]], axis=0)
    for k, n_ref in enumerate((n0, n1, n2, n3)):
        n_ref[...] = norm(kept[y ^ k], g_ref[...]).astype(BF)
    r0[...] = kept[q]
    r1[...] = kept[q ^ 1]
    r23[:SLICE] = kept[q ^ 2]
    r23[SLICE:] = kept[q ^ 3]


SCALAR = pl.BlockSpec(memory_space=pltpu.SMEM)
NEAR = pl.BlockSpec(memory_space=pltpu.VMEM)
PARAMS = pltpu.CompilerParams(vmem_limit_bytes=24 * 1024 * 1024)


def cost(flops, moved):
    return pl.CostEstimate(flops=flops, bytes_accessed=moved, transcendentals=0)


FRAMES = pltpu.VMEM((6, ROWS, WIDE, C), BF)
EDGES = pltpu.VMEM((2, 6, WIDE, C), BF)
ACC = pltpu.VMEM((4 * WIDE, ROWS * 3 * C), F32)
PART = jax.ShapeDtypeStruct((ROWS, 4 * WIDE, C), F32)
EDGE = jax.ShapeDtypeStruct((6, WIDE, C), BF)
HIDDEN = jax.ShapeDtypeStruct((4, ROWS, WIDE, C), BF)
UNIT = 2 * 4 * WIDE * 3 * C * 3 * C


def conv_call(kernel, args, scalars, out_shape, scratch, share, name):
    return pl.pallas_call(
        kernel,
        out_shape=out_shape,
        in_specs=[SCALAR] * scalars + [NEAR] * (len(args) - scalars),
        out_specs=jax.tree.map(lambda _: NEAR, out_shape),
        scratch_shapes=scratch,
        compiler_params=PARAMS,
        cost_estimate=cost(share * UNIT, 6_000_000),
        name=name,
    )(*args)


def project(raw, wq_ref, wkv_ref):
    queries = jnp.dot(raw, wq_ref[...], preferred_element_type=F32).astype(BF)
    queries = lax.dot_general(
        queries, wkv_ref[:, :C], (((1,), (1,)), ((), ())), preferred_element_type=F32
    )
    return (queries * SCALE).astype(BF)


def score(queries, keys):
    return lax.dot_general(queries, keys, (((1,), (1,)), ((), ())), preferred_element_type=F32)


def sweep(queries, keys, acc, state):
    rows = queries.shape[0]
    if state is None:
        peak = jnp.full((rows, 1), -1e30, F32)
        total = jnp.zeros((rows, 1), F32)
        acc[...] = jnp.zeros((rows, C), F32)
    else:
        peak, total = state
    scores = score(queries, keys[0][...])
    for i, block in enumerate(keys):
        following = score(queries, keys[i + 1][...]) if i + 1 < len(keys) else None
        risen = jnp.maximum(peak, jnp.max(scores, axis=1, keepdims=True))
        share = jnp.exp2(peak - risen)
        e = jnp.exp2(scores - risen)
        total = total * share + jnp.sum(e, axis=1, keepdims=True)
        acc[...] = acc[...] * share + jnp.dot(
            e.astype(BF), block[...], preferred_element_type=F32
        )
        peak, scores = risen, following
    return peak, total


def noted(peak, total):
    rows = peak.shape[0]
    return jnp.concatenate(
        [jnp.broadcast_to(peak, (rows, 128)), jnp.broadcast_to(total, (rows, 128))], axis=1
    )


def recalled(stats):
    return (
        jnp.max(stats[:, :128], axis=1, keepdims=True),
        jnp.max(stats[:, 128:], axis=1, keepdims=True),
    )


def diagonal():
    row = lax.broadcasted_iota(jnp.int32, (HALF, C), 0)
    return row == lax.broadcasted_iota(jnp.int32, (HALF, C), 1)


def packed(peak, total, weighted):
    level = peak + jnp.log2(total)
    place = lax.broadcasted_iota(jnp.int32, (16, C), 0)
    tail = jnp.zeros((16, C), F32)
    for half in range(2):
        column = level[half * HALF : (half + 1) * HALF]
        line = jnp.sum(jnp.where(diagonal(), column, 0.0), axis=0, keepdims=True)
        first = line.astype(BF).astype(F32)
        second = (line - first).astype(BF).astype(F32)
        for p, piece in enumerate((first, second, line - first - second)):
            tail = jnp.where(place == 2 * p + half, piece, tail)
    return jnp.concatenate([(weighted / total).astype(BF), tail.astype(BF)], axis=0)


def level_of(part):
    tail = part[BLOCK:].astype(F32)
    place = lax.broadcasted_iota(jnp.int32, (16, C), 0)
    columns = []
    for half in range(2):
        line = jnp.sum(jnp.where(place % 2 == half, tail, 0.0), axis=0, keepdims=True)
        columns.append(jnp.sum(jnp.where(diagonal(), line, 0.0), axis=1, keepdims=True))
    return jnp.concatenate(columns, axis=0)


def attend_near_kernel(qa, qb, k0, k1, k2, k3, wq, wkv, out, stats, ready):
    queries = project(jnp.concatenate([qa[...], qb[...]], axis=0), wq, wkv)
    ready[...] = queries
    stats[...] = noted(*sweep(queries, (k0, k1, k2, k3), out, None))


def attend_far_kernel(ready, weighted, stats, k0, k1, out_a, out_b, acc):
    acc[...] = weighted[...]
    peak, total = sweep(ready[...], (k0, k1), acc, recalled(stats))
    out_a[...] = packed(peak[:BLOCK], total[:BLOCK], acc[:BLOCK])
    out_b[...] = packed(peak[BLOCK:], total[BLOCK:], acc[BLOCK:])


def attend_all_kernel(q, k0, k1, k2, k3, k4, k5, k6, k7, wq, wkv, out, acc):
    queries = project(q[...], wq, wkv)
    peak, total = sweep(queries, (k0, k1, k2, k3, k4, k5, k6, k7), acc, None)
    out[...] = packed(peak, total, acc[...])


def attend_own_kernel(q, k0, k1, wq, wkv, out, stats, ready):
    queries = project(q[...], wq, wkv)
    ready[...] = queries
    stats[...] = noted(*sweep(queries, (k0, k1), out, None))


def attend_more_kernel(ready, weighted, before, k0, k1, out, stats):
    out[...] = weighted[...]
    stats[...] = noted(*sweep(ready[...], (k0, k1), out, recalled(before)))


def attend_rest_kernel(ready, weighted, stats, k0, k1, k2, k3, k4, k5, out, acc):
    acc[...] = weighted[...]
    peak, total = sweep(ready[...], (k0, k1, k2, k3, k4, k5), acc, recalled(stats))
    out[...] = packed(peak, total, acc[...])


def attend(kernel, first, keys, weights, out_shape, scratch, flops, name):
    args = list(first) + list(keys) + list(weights)
    return pl.pallas_call(
        kernel,
        out_shape=out_shape,
        in_specs=[NEAR] * len(args),
        out_specs=[NEAR] * len(out_shape),
        scratch_shapes=scratch,
        compiler_params=PARAMS,
        cost_estimate=cost(flops // 8, 2 * BLOCK * C),
        name=name,
    )(*args)


def levels_of(parts):
    return [level_of(p) for p in parts]


def merge_first_kernel(p0, p1, out, stats):
    levels = levels_of((p0, p1))
    peak = jnp.maximum(*levels)
    shares = [jnp.exp2(level - peak) for level in levels]
    out[...] = p0[:BLOCK].astype(F32) * shares[0] + p1[:BLOCK].astype(F32) * shares[1]
    stats[...] = noted(peak, shares[0] + shares[1])


def merge_first_call(own, across):
    return pl.pallas_call(
        merge_first_kernel,
        in_specs=[NEAR] * 2,
        out_specs=[NEAR] * 2,
        out_shape=[
            jax.ShapeDtypeStruct((BLOCK, C), F32),
            jax.ShapeDtypeStruct((BLOCK, 256), F32),
        ],
        compiler_params=PARAMS,
        name="merge_first",
    )(own, across)


def merge_kernel(at_ref, weighted, stats, p2, p3, wkv_ref, out_a, out_b):
    parts = (p2, p3)
    begun, total = recalled(stats)
    levels = levels_of(parts)
    peak = jnp.maximum(begun, jnp.maximum(*levels))
    share = jnp.exp2(begun - peak)
    mixed, total = weighted[...] * share, total * share
    for part, level in zip(parts, levels):
        share = jnp.exp2(level - peak)
        mixed += part[:BLOCK].astype(F32) * share
        total += share
    mixed = mixed / total
    y = jnp.dot(mixed.astype(BF), wkv_ref[:, C:], preferred_element_type=F32)
    even = jnp.concatenate([y[:SLICE], y[2 * SLICE : 3 * SLICE]], axis=0)
    odd = jnp.concatenate([y[SLICE : 2 * SLICE], y[3 * SLICE :]], axis=0)
    core = at_ref[3]
    out_a[...] = jnp.where(core == 0, even, odd).astype(BF)
    out_b[...] = jnp.where(core == 0, odd, even).astype(BF)


def merge_call(at, parts, wkv):
    return pl.pallas_call(
        merge_kernel,
        in_specs=[SCALAR] + [NEAR] * 5,
        out_specs=[NEAR] * 2,
        out_shape=[jax.ShapeDtypeStruct((HALF, C), BF)] * 2,
        compiler_params=PARAMS,
        name="merge",
    )(at, *parts, wkv)


def final_kernel(at_ref, a_ref, b_ref, r0, ry, rc, wo_ref, out_ref, parts):
    frame, low = at_ref[0], at_ref[4]
    ya = jnp.dot(a_ref[...], wo_ref[...], preferred_element_type=F32)
    yb = jnp.dot(b_ref[...], wo_ref[...], preferred_element_type=F32)
    even, odd = jnp.where(low == 0, ya, yb), jnp.where(low == 0, yb, ya)
    parts[0] = even[:SLICE] + r0[...]
    parts[1] = odd[:SLICE] + rc[:SLICE]
    parts[2] = even[SLICE:] + ry[:SLICE]
    parts[3] = odd[SLICE:] + rc[SLICE:]
    for q in range(4):
        part = parts[frame ^ q]
        out_ref[0, 0, q * COLS : (q + 1) * COLS] = part[:COLS]
        out_ref[0, 1, q * COLS : (q + 1) * COLS] = part[COLS:]


def final_call(at, a, b, r0, ry, rc, wo):
    return pl.pallas_call(
        final_kernel,
        in_specs=[SCALAR] + [NEAR] * 6,
        out_specs=NEAR,
        out_shape=jax.ShapeDtypeStruct((1, ROWS, 4 * COLS, C), F32),
        scratch_shapes=[pltpu.VMEM((4, SLICE, C), F32)],
        compiler_params=PARAMS,
        name="final",
    )(at, a, b, r0, ry, rc, wo)


def shards(
    latent, cache_first, cache_second, gain_first, conv_first, gain_second, conv_second,
    gain_attention, query_weight, keyvalue_weight, out_weight,
):
    low, high, core = (lax.axis_index(a) for a in ("yl", "yh", "c"))
    member = high * 2 + core
    odd = lax.axis_index("z") % 2
    at = jnp.stack([member, odd, high * 2 + low, core, low]).astype(jnp.int32)

    both = jax.ShapeDtypeStruct((ROWS, WIDE, C), BF)
    two = jax.ShapeDtypeStruct((2, ROWS, WIDE, C), BF)
    held = [pltpu.VMEM((4, ROWS, WIDE, C), BF)]
    pieces, near, far = conv_call(
        pieces_kernel, (at, latent), 1, [both, both, two], held, 0, "pieces"
    )
    yo = send(far, ("yh",), other("yh"))
    caches = conv_call(
        caches_kernel, (at, cache_first, cache_second), 1, HIDDEN, held, 0, "caches"
    )
    near, caches = lax.optimization_barrier((near, caches))
    co = conv_call(relay_kernel, (near, yo), 0, two, [], 0, "relay")
    co = send(co, ("c",), other("c"))

    a, b = conv_call(edges_kernel, (at, pieces, yo, co, caches), 1, [EDGE, EDGE], [], 0, "edges")
    a = send(a, AXES, row_swap(False))
    b = send(b, AXES, row_swap(True))
    gain1, gain2, gain3 = gain_first, gain_second, gain_attention
    part = conv_call(
        first_inner_kernel, (at, pieces, yo, co, caches, gain1, conv_first), 1, PART,
        [FRAMES, ACC], 6, "first_inner",
    )
    hidden, ha, hb = conv_call(
        first_outer_kernel, (at, part, a, b, caches, gain1, gain2, conv_first), 1,
        [HIDDEN, EDGE, EDGE], [EDGES], 2, "first_outer",
    )
    ha = send(ha, AXES, row_swap(False))
    hb = send(hb, AXES, row_swap(True))
    part = conv_call(
        second_inner_kernel, (hidden, caches, conv_second), 0, PART, [FRAMES, ACC], 6,
        "second_inner",
    )
    slice_of = lambda n, kind: jax.ShapeDtypeStruct((n * SLICE, C), kind)
    n0, n1, n2, n3, r0, r1, r23 = conv_call(
        second_outer_kernel,
        (at, part, ha, hb, pieces, yo, co, gain3, conv_second), 1,
        [slice_of(1, BF)] * 4 + [slice_of(1, F32)] * 2 + [slice_of(2, F32)],
        [EDGES, pltpu.VMEM((4, ROWS, WIDE, C), F32), pltpu.VMEM((4, SLICE, C), F32)], 2,
        "second_outer",
    )

    group = ("yl", "yh")
    block = jnp.concatenate([n0] + [send(n, group, to_plane(k + 1)) for k, n in enumerate((n1, n2, n3))])
    lines = ("x", "z", "c")
    cross = lambda v: send(v, ("c",), other("c"))
    keyed = lambda v, turn: send(v, lines, line_swap(turn, True))
    asked = lambda v, turn: send(v, lines, line_swap(turn, False))
    p0 = block
    a0, b0 = keyed(p0, False), keyed(p0, True)
    qa, qb = asked(p0, False), asked(p0, True)
    p1 = cross(p0)
    ab, qo = keyed(a0, True), asked(qb, False)
    a1, b1 = cross(qa), cross(qb)
    weights = (query_weight, keyvalue_weight)

    near_keys = [p0, p1, a0, b0]
    unit = 4 * BLOCK * BLOCK * C
    wide = jax.ShapeDtypeStruct((BLOCK + 16, C), BF)
    queried = lambda n: jax.ShapeDtypeStruct((n * BLOCK, C), BF)
    begun = lambda n: [
        jax.ShapeDtypeStruct((n * BLOCK, C), F32),
        jax.ShapeDtypeStruct((n * BLOCK, 256), F32),
    ]
    after = lambda v, mark: lax.optimization_barrier((v, mark))[0]
    own_weighted, own_stats, own_ready = attend(
        attend_own_kernel, [p0], [p0, p1], weights, begun(1) + [queried(1)], [], 2 * unit,
        "attend_own",
    )
    weighted, stats, ready = attend(
        attend_near_kernel, [after(qa, own_stats), qb], near_keys, weights,
        begun(2) + [queried(2)], [], 8 * unit, "attend_near",
    )
    ba = cross(after(qo, stats))
    ry = send(after(r23, stats), ("yh",), other("yh"))
    weighted, stats = attend(
        attend_more_kernel, [ready, weighted, stats], [a1, b1], [], begun(2),
        [], 4 * unit, "attend_more",
    )
    (to,) = attend(
        attend_all_kernel, [after(qo, stats)], near_keys + [a1, b1, ab, ba], weights, [wide],
        [pltpu.VMEM((BLOCK, C), F32)], 8 * unit, "attend_across",
    )
    sa, sb = attend(
        attend_far_kernel, [after(ready, (to, ry)), weighted, stats], [ab, ba], [],
        [wide] * 2, [pltpu.VMEM((2 * BLOCK, C), F32)], 4 * unit, "attend_far",
    )
    (own,) = attend(
        attend_rest_kernel, [after(own_ready, sa), own_weighted, own_stats],
        [a0, b0, a1, b1, ab, ba], [], [wide],
        [pltpu.VMEM((BLOCK, C), F32)], 6 * unit, "attend_rest",
    )
    to = send(to, lines, line_across)
    rc_from = after(ry, sa)
    sa, sb = asked(sa, False), asked(sb, True)
    rc = cross(jnp.concatenate([r1, rc_from[SLICE:]]))
    to_a, to_b = merge_call(at, (*merge_first_call(own, to), sa, sb), keyvalue_weight)
    home = ("yl", "c")
    to_a, to_b = send(to_a, home, to_home(0)), send(to_b, home, to_home(1))
    return final_call(at, to_a, to_b, r0, ry, rc, out_weight)


def solution(mesh):
    fine = Mesh(mesh.devices.reshape([SIZES[a] for a in AXES]), AXES)
    frames, rows = ("yh", "c"), ("x", "yl", "z")
    in_specs = (P(frames, rows), P(None, rows), P(None, rows)) + (P(),) * 8
    return jax.shard_map(
        shards, mesh=fine, in_specs=in_specs, out_specs=P(frames, rows), check_vma=False
    )
```
